32 devices in a mesh: band: 32 (over z, y, x, core).
Axes of the slice: x: 2, y: 2, z: 4, core: 2. Of those that a mesh axis runs over, the one named last changes fastest.
Arguments:
- grid_features: bfloat16 [98304, 1024], P('band'), may hold values from -6 to 6
- mesh_features: bfloat16 [8192, 1024], P('band'), may hold values from -102 to 102
- sources: int32 [8192, 12], P('band'), may hold values from 0 to 98303, as said below
- window_shift: int32 [1], replicated, may hold values from 1 to 127
- w_query: bfloat16 [1024, 1024], replicated, may hold values from -0.1875 to 0.1875
- w_grid_kv: bfloat16 [1024, 2048], replicated, may hold values from -0.1875 to 0.1875
- w_enc_out: bfloat16 [1024, 1024], replicated, may hold values from -0.1875 to 0.1875
- norm_gain: float32 [1024], replicated, may hold values from 0.5 to 1.5
- w_win_qkv: bfloat16 [1024, 3072], replicated, may hold values from -0.1875 to 0.1875
- w_win_out: bfloat16 [1024, 1024], replicated, may hold values from -0.1875 to 0.1875
- head_scale: float32 [16], replicated, may hold values from 0.5 to 48
Outputs:
- mixed: bfloat16 [8192, 1024], P('band')
The draws below stay inside these ranges and needn't reach their ends.
Inputs may be any that keep to these rules, and one draw needn't show every extreme that they name: `sources`: mesh node m of band b = m // 256 names grid points of its own band, b * 3072 to (b + 1) * 3072 - 1, unless it is among the first or the last 16 nodes of its band; those name points from b * 3072 - 384 to (b + 1) * 3072 + 383, cut to the grid, the first ones never above their own band and the last ones never below it. In every band both ends of that range are named where they lie in the grid.
All inputs are finite; a program needn't handle non-finite values.
Results may differ from the reference program's by a relative error of at most 0.01.
Values may be sent and summed in bfloat16 or wider, within the bound.
No kernel may reach another device: no remote copies, remote signals or barrier semaphores. Data moves between devices by JAX's collectives and lax.ppermute only.
A program may use at most 192 MiB of HBM per device.

```python
import math
import jax
import jax.numpy as jnp
from jax import lax

HEADS = 16
HEAD_FEATURES = 64
D = 1024
EDGES = 12
WIN = 128
M_DEV = 256
G_DEV = 3072
REACH = 384
QRIM = 16
MESH = 8192
GRID = 98304


def draw_sources(key, part):
    key = jax.random.fold_in(key, 1)
    near_key, low_key, high_key = jax.random.split(key, 3)
    nodes = jnp.arange(MESH, dtype=jnp.int32)
    band_index = nodes // M_DEV
    within = nodes % M_DEV
    ratio = G_DEV // M_DEV
    band_low = band_index * G_DEV
    band_high = band_low + G_DEV - 1
    center = band_low + within * ratio
    near = center[:, None] + jax.random.randint(near_key, (MESH, EDGES), -2 * ratio, 2 * ratio + 1, dtype=jnp.int32)
    near = jnp.clip(near, band_low[:, None], band_high[:, None])
    lower = band_low[:, None] + jax.random.randint(low_key, (MESH, EDGES), -REACH, REACH // 4, dtype=jnp.int32)
    upper = band_high[:, None] + 1 + jax.random.randint(high_key, (MESH, EDGES), -(REACH // 4), REACH, dtype=jnp.int32)
    lower = lower.at[:, 0].set(jnp.where(within == 0, band_low - REACH, lower[:, 0]))
    upper = upper.at[:, 0].set(jnp.where(within == M_DEV - 1, band_high + REACH, upper[:, 0]))
    chosen = jnp.where((within < QRIM)[:, None], lower, jnp.where((within >= M_DEV - QRIM)[:, None], upper, near))
    chosen = jnp.clip(chosen, 0, GRID - 1)
    return chosen.astype(jnp.int32)


def draw_mesh_features(key, part):
    key = jax.random.fold_in(key, 2)
    value_key = jax.random.fold_in(key, 0)
    values = jnp.clip(jax.random.normal(value_key, (MESH, D), jnp.float32), -6.0, 6.0)
    return values.astype(jnp.bfloat16)


def draw_head_scale(key, part):
    key = jax.random.fold_in(key, 3)
    logs = jax.random.uniform(key, (HEADS,), jnp.float32, jnp.log(0.5), jnp.log(4.0))
    return jnp.exp(logs).astype(jnp.float32)


def block_scale(own_key, extent, pieces, low, high):
    level = 1.0
    for axis_at, shards_of in pieces:
        steps = jax.random.uniform(jax.random.fold_in(jax.random.fold_in(own_key, 6), axis_at), (shards_of,), jnp.float32, low / len(pieces), high / len(pieces))
        level = level * jnp.repeat(jnp.exp(steps), extent[axis_at] // shards_of).reshape((-1,) + (1,) * (len(extent) - 1 - axis_at))
    return level


def scatter_about(own_key, shape, scale, most, cuts=(), kind=jnp.bfloat16):
    values = scale * jax.random.normal(own_key, shape, jnp.float32)
    if cuts:
        values = values * block_scale(own_key, shape, cuts, -0.22, 0.18)
    return jnp.clip(values, -most, most).astype(kind)


def setup_inputs(seed: int = 0) -> dict:
    key_list = jax.random.split(jax.random.key(seed), 12)
    grid_features = scatter_about(key_list[0], (GRID, D), 1.0, 6.0, ((0, 32),))
    mesh_features = draw_mesh_features(jax.random.fold_in(key_list[11], 71), 0)
    sources = draw_sources(jax.random.fold_in(key_list[11], 71), 0)
    window_shift = jax.random.randint(key_list[3], (1,), 1, WIN).astype(jnp.int32)
    w_query = scatter_about(key_list[4], (D, D), D ** -0.5, 0.1875)
    w_grid_kv = scatter_about(key_list[5], (D, 2 * D), D ** -0.5, 0.1875)
    w_enc_out = scatter_about(key_list[6], (D, D), D ** -0.5, 0.1875)
    norm_gain = jnp.clip(1.0 + 0.1 * jax.random.normal(key_list[7], (D,), jnp.float32), 0.5, 1.5)
    w_win_qkv = scatter_about(key_list[8], (D, 3 * D), D ** -0.5, 0.1875)
    w_win_out = scatter_about(key_list[9], (D, D), D ** -0.5, 0.1875)
    head_scale = draw_head_scale(jax.random.fold_in(key_list[11], 71), 0)
    return {"grid_features": grid_features, "mesh_features": mesh_features, "sources": sources, "window_shift": window_shift, "w_query": w_query, "w_grid_kv": w_grid_kv, "w_enc_out": w_enc_out, "norm_gain": norm_gain, "w_win_qkv": w_win_qkv, "w_win_out": w_win_out, "head_scale": head_scale}


def layer_norm(values, norm_gain):
    wide = values.astype(jnp.float32)
    center = lax.optimization_barrier(jnp.mean(wide, axis=-1, keepdims=True))
    spread = lax.optimization_barrier(jnp.mean((wide - center) ** 2, axis=-1, keepdims=True))
    return ((wide - center) / jnp.sqrt(spread + 1e-05) * norm_gain).astype(jnp.bfloat16)

def reference(grid_features, mesh_features, sources, window_shift, w_query, w_grid_kv, w_enc_out, norm_gain, w_win_qkv, w_win_out, head_scale):
    grid_kv = jnp.dot(grid_features, w_grid_kv, preferred_element_type=jnp.float32).astype(jnp.bfloat16)
    queries = jnp.dot(mesh_features, w_query, preferred_element_type=jnp.float32).astype(jnp.bfloat16)
    blocks = MESH // M_DEV

    def encode(pair):
        query_block, source_block = pair
        picked = grid_kv[source_block.reshape(-1)].reshape(M_DEV, EDGES, 2 * D)
        key_row_block = picked[:, :, :D].reshape(M_DEV, EDGES, HEADS, HEAD_FEATURES).astype(jnp.float32)
        value_row_block = picked[:, :, D:].reshape(M_DEV, EDGES, HEADS, HEAD_FEATURES).astype(jnp.float32)
        query_head_split = query_block.reshape(M_DEV, HEADS, HEAD_FEATURES).astype(jnp.float32)
        logit_scores = jnp.einsum('qka,qfka->qfk', query_head_split, key_row_block) / math.sqrt(HEAD_FEATURES)
        attention_weights = jax.nn.softmax(logit_scores, axis=1).astype(jnp.bfloat16)
        summed_values = jnp.einsum('uys,uysz->usz', attention_weights.astype(jnp.float32), value_row_block)
        return summed_values.astype(jnp.bfloat16).reshape(M_DEV, D)
    gathered = lax.map(encode, (queries.reshape(blocks, M_DEV, D), sources.reshape(blocks, M_DEV, EDGES)))
    gathered = gathered.reshape(MESH, D)
    mesh_mid = (mesh_features.astype(jnp.float32) + jnp.dot(gathered, w_enc_out, preferred_element_type=jnp.float32)).astype(jnp.bfloat16)
    normed = layer_norm(mesh_mid, norm_gain)
    offset = window_shift[0]
    rolled = jnp.roll(normed, -offset, axis=0)
    win_qkv = jnp.dot(rolled, w_win_qkv, preferred_element_type=jnp.float32).astype(jnp.bfloat16)
    grouped = win_qkv.reshape(MESH // WIN, WIN, 3, HEADS, HEAD_FEATURES).astype(jnp.float32)
    logit_scores = jnp.einsum('wqhd,wkhd->whqk', grouped[:, :, 0], grouped[:, :, 1])
    logit_scores = logit_scores * head_scale[None, :, None, None] / math.sqrt(HEAD_FEATURES)
    probs = jax.nn.softmax(logit_scores, axis=-1).astype(jnp.bfloat16)
    win_out = jnp.einsum('whqk,wkhd->wqhd', probs.astype(jnp.float32), grouped[:, :, 2]).astype(jnp.bfloat16)
    win_out = jnp.roll(win_out.reshape(MESH, D), offset, axis=0)
    mixed = mesh_mid.astype(jnp.float32) + jnp.dot(win_out, w_win_out, preferred_element_type=jnp.float32)
    return mixed.astype(jnp.bfloat16)
```

```python
import jax
import jax.numpy as jnp
from jax import lax
from jax.experimental import pallas as pl
from jax.experimental.pallas import tpu as pltpu
from jax.sharding import PartitionSpec as P

WIN = 128
REACH = 384
RIM = 16
HEAD = 64
QUAD = 256
LANES = 128
NEG = -1e30

BF16 = jnp.bfloat16
F32 = jnp.float32


def dot(a, b):
    return jnp.dot(a, b, preferred_element_type=F32)


def dot_t(a, b):
    return lax.dot_general(a, b, (((1,), (1,)), ((), ())), preferred_element_type=F32)


def layer_norm(mid, gain):
    wide = mid.astype(F32)
    center = jnp.mean(wide, axis=-1, keepdims=True)
    spread = jnp.mean((wide - center) ** 2, axis=-1, keepdims=True)
    return ((wide - center) / jnp.sqrt(spread + 1e-05) * gain).astype(BF16)


def spread_rows(rows_ref, first, table_ref, at):
    lines = rows_ref.shape[1] // LANES
    rows = rows_ref[pl.ds(first, 16), :].astype(F32)
    for c in range(lines):
        table_ref[pl.ds(at + c, 16, lines), :] = rows[:, c * LANES : (c + 1) * LANES]


def collect(src_ref, first, table_ref, tiles_ref, edges_ref):
    count, width = edges_ref.shape
    lines = width // LANES
    for j in range(count):
        at = pl.multiple_of(src_ref[first + j], lines)
        tiles_ref[j * lines : (j + 1) * lines, :] = table_ref[pl.ds(at, lines), :]
    for c in range(lines):
        part = tiles_ref[pl.ds(c, count, lines), :]
        edges_ref[:, c * LANES : (c + 1) * LANES] = part.astype(BF16)


def attend_edges(queries, edges, neg_ref):
    scores = dot_t(queries, edges) + neg_ref[...]
    top = jnp.max(scores, axis=-1, keepdims=True)
    grown = jnp.exp(scores - top)
    weights = (grown / jnp.sum(grown, axis=-1, keepdims=True)).astype(BF16)
    return dot(weights, edges).astype(BF16)


def fill_mask(neg_ref, edge_count):
    shape = neg_ref.shape
    row_node = lax.broadcasted_iota(jnp.int32, shape, 0) % RIM
    col = lax.broadcasted_iota(jnp.int32, shape, 1)
    inside = (col >= row_node * edge_count) & (col < (row_node + 1) * edge_count)
    neg_ref[...] = jnp.where(inside, 0.0, NEG)


def project_heads(pool, w_ref, out_ref, quad):
    per, rows, width = pool.shape
    cols = pl.ds(pl.multiple_of(quad * QUAD, QUAD), QUAD)
    wide = dot(pool.reshape(per * rows, width), w_ref[:, cols])
    head = lax.broadcasted_iota(jnp.int32, (rows, QUAD), 1) // HEAD
    total = wide[:rows]
    for j in range(1, per):
        total = jnp.where(head == j, wide[j * rows : (j + 1) * rows], total)
    out_ref[:, cols] = total.astype(BF16)


def interior_kernel(
    src_ref, x_hbm, mesh_ref, wq_hbm, wkv_hbm, we_hbm, gain_ref,
    mid_ref, norm_ref, qrim_ref, xrim_ref,
    xb, table, pool, wq, wk, wv, we, qs, tiles0, tiles1, edges0, edges1, neg, gathered, sems,
):
    grid_rows, width = xb.shape
    mesh_rows = mesh_ref.shape[0]
    heads = pool.shape[0]
    lines = width // LANES
    quads = width // QUAD
    group_edges = edges0.shape[0]
    groups = mesh_rows // RIM
    chunk = 512
    chunks = grid_rows // chunk

    def load(source, target, sem):
        copy = pltpu.make_async_copy(source, target, sems.at[sem])
        copy.start()
        return copy

    get_wq = load(wq_hbm, wq, 0)
    get_wk = load(wkv_hbm.at[:, 0:width], wk, 1)
    get_x = [
        load(x_hbm.at[pl.ds(c * chunk, chunk)], xb.at[pl.ds(c * chunk, chunk)], 4 + c)
        for c in range(chunks)
    ]
    get_wv = load(wkv_hbm.at[:, width : 2 * width], wv, 2)
    get_we = load(we_hbm, we, 3)
    fill_mask(neg, group_edges // RIM)

    get_wq.wait()

    def query_step(n, carry):
        cols = pl.ds(pl.multiple_of(n * QUAD, QUAD), QUAD)
        qs[:, cols] = dot(mesh_ref[...], wq[:, cols]).astype(BF16) * BF16(0.125)
        return carry

    lax.fori_loop(0, quads, query_step, 0)
    get_wk.wait()

    def key_step(t, carry):
        cols = pl.ds(pl.multiple_of(t * QUAD, QUAD), QUAD)
        queries = qs[:, cols]
        keys = wk[:, cols]
        head = lax.broadcasted_iota(jnp.int32, queries.shape, 1) // HEAD
        for j in range(4):
            own = jnp.where(head == j, queries, BF16(0))
            pool[t * 4 + j] = dot_t(own, keys).astype(BF16)
        return carry

    lax.fori_loop(0, quads, key_step, 0)

    for c in range(chunks):
        get_x[c].wait()

        def spread_step(i, carry, c=c):
            first = pl.multiple_of(c * chunk + i * 16, 16)
            spread_rows(xb, first, table, first * lines)
            return carry

        lax.fori_loop(0, chunk // 16, spread_step, 0, unroll=2)

    def gather(group, tiles, edges):
        collect(src_ref, group * group_edges, table, tiles, edges)

    def attend(group, edges):
        rows = pl.ds(pl.multiple_of(group * RIM, RIM), RIM)
        queries = pool[:, rows, :].reshape(heads * RIM, width)
        pool[:, rows, :] = attend_edges(queries, edges[...], neg).reshape(heads, RIM, width)

    for side, group in enumerate((0, groups - 1)):
        gather(group, tiles0 if side == 0 else tiles1, xrim_ref.at[side])
        qrim_ref[side] = pool[:, group * RIM : (group + 1) * RIM, :].reshape(heads * RIM, width)

    gather(1, tiles0, edges0)

    def group_step(i, carry):
        group = 1 + 2 * i
        gather(group + 1, tiles1, edges1)
        attend(group, edges0)
        gather(jnp.minimum(group + 2, groups - 1), tiles0, edges0)
        attend(group + 1, edges1)
        return carry

    lax.fori_loop(0, (groups - 2) // 2, group_step, 0)

    get_wv.wait()

    def value_step(t, carry):
        project_heads(pool[pl.ds(t * 4, 4)], wv, gathered, t)
        return carry

    lax.fori_loop(0, quads, value_step, 0)
    get_we.wait()

    def out_step(n, carry):
        cols = pl.ds(pl.multiple_of(n * QUAD, QUAD), QUAD)
        total = mesh_ref[:, cols].astype(F32) + dot(gathered[...], we[:, cols])
        mid_ref[:, cols] = total.astype(BF16)
        return carry

    lax.fori_loop(0, quads, out_step, 0)
    norm_ref[...] = layer_norm(mid_ref[...], gain_ref[...])


def rim_kernel(
    src_ref, shift_ref, low_ref, high_ref, qrim_ref, xrim_ref, mesh_ref, wkv_hbm, we_hbm, gain_ref,
    mid_in, norm_in,
    mid_ref, ac_ref, b_ref,
    table0, table1, tiles0, tiles1, edges0, edges1, pool, wv, we, neg, gathered, sems,
):
    width = mesh_ref.shape[1]
    mesh_rows = mesh_ref.shape[0]
    heads = pool.shape[0]
    lines = width // LANES
    quads = width // QUAD
    group_edges = edges0.shape[0]
    get_wv = pltpu.make_async_copy(wkv_hbm.at[:, width : 2 * width], wv, sems.at[0])
    get_wv.start()
    get_we = pltpu.make_async_copy(we_hbm, we, sems.at[1])
    get_we.start()
    fill_mask(neg, group_edges // RIM)

    def spread_halo(i, carry):
        first = pl.multiple_of(i * 16, 16)
        spread_rows(low_ref, first, table0, first * lines)
        spread_rows(high_ref, first, table1, first * lines)
        return carry

    lax.fori_loop(0, REACH // 16, spread_halo, 0, unroll=2)

    def spread_own(i, carry):
        first = pl.multiple_of(i * 16, 16)
        spread_rows(xrim_ref.at[0], first, table0, (REACH + first) * lines)
        spread_rows(xrim_ref.at[1], first, table1, (REACH + first) * lines)
        return carry

    lax.fori_loop(0, group_edges // 16, spread_own, 0, unroll=2)
    parts = ((table0, tiles0, edges0), (table1, tiles1, edges1))
    for side, (table, tiles, edges) in enumerate(parts):
        collect(src_ref, side * group_edges, table, tiles, edges)
        pooled = attend_edges(qrim_ref[side], edges[...], neg)
        pool[:, side * RIM : (side + 1) * RIM, :] = pooled.reshape(heads, RIM, width)
    get_wv.wait()

    def value_step(t, carry):
        project_heads(pool[pl.ds(t * 4, 4)], wv, gathered, t)
        return carry

    lax.fori_loop(0, quads, value_step, 0)
    get_we.wait()
    edge_mesh = jnp.concatenate([mesh_ref[:RIM], mesh_ref[mesh_rows - RIM :]], axis=0)
    rim_mid = (edge_mesh.astype(F32) + dot(gathered[...], we[...])).astype(BF16)
    rim_norm = layer_norm(rim_mid, gain_ref[...])
    mid_ref[RIM : mesh_rows - RIM] = mid_in[RIM : mesh_rows - RIM]
    mid_ref[:RIM] = rim_mid[:RIM]
    mid_ref[mesh_rows - RIM :] = rim_mid[RIM:]
    tile0 = jnp.concatenate([rim_norm[:RIM], norm_in[RIM:WIN]], axis=0)
    tile1 = jnp.concatenate([norm_in[WIN : mesh_rows - RIM], rim_norm[RIM:]], axis=0)
    first = lax.broadcasted_iota(jnp.int32, tile0.shape, 0) < shift_ref[0]
    ac_ref[...] = jnp.where(first, tile0, tile1)
    b_ref[...] = jnp.where(first, tile1, tile0)


def soft_rows(scores):
    top = jnp.max(scores, axis=-1, keepdims=True)
    grown = jnp.exp(scores - top)
    return (grown / jnp.sum(grown, axis=-1, keepdims=True)).astype(BF16)


def pair_queries(queries):
    second = lax.broadcasted_iota(jnp.int32, queries.shape, 1) >= HEAD
    zero = BF16(0)
    return jnp.concatenate(
        [jnp.where(second, zero, queries), jnp.where(second, queries, zero)], axis=0
    )


def pair_scale(scale_ref, pair, shape):
    upper = lax.broadcasted_iota(jnp.int32, shape, 0) >= shape[0] // 2
    return jnp.where(upper, scale_ref[2 * pair + 1], scale_ref[2 * pair]) * 0.125


def join_pair(wide):
    rows = wide.shape[0] // 2
    second = lax.broadcasted_iota(jnp.int32, (rows, wide.shape[1]), 1) >= HEAD
    return jnp.where(second, wide[rows:], wide[:rows]).astype(BF16)


def inner_kernel(scale_ref, ac_ref, b_ref, w_hbm, ac_out, out_ref, w, qkv, sems):
    width = ac_ref.shape[1]
    copies = []
    for c in range(3):
        cols = slice(c * width, (c + 1) * width)
        copy = pltpu.make_async_copy(w_hbm.at[:, cols], w.at[c], sems.at[c])
        copy.start()
        copies.append(copy)
    rows = jnp.concatenate([ac_ref[...], b_ref[...]], axis=0)
    for c in range(3):
        copies[c].wait()

        def step(n, carry, c=c):
            cols = pl.ds(pl.multiple_of(n * QUAD, QUAD), QUAD)
            part = dot(rows, w[c, :, cols]).astype(BF16)
            ac_out[c, :, cols] = part[:WIN]
            qkv[c, :, cols] = part[WIN:]
            return carry

        lax.fori_loop(0, width // QUAD, step, 0)

    def pair_step(pair, carry):
        cols = pl.ds(pl.multiple_of(pair * LANES, LANES), LANES)
        scores = dot_t(pair_queries(qkv[0, :, cols]), qkv[1, :, cols])
        probs = soft_rows(scores * pair_scale(scale_ref, pair, scores.shape))
        out_ref[:, cols] = join_pair(dot(probs, qkv[2, :, cols]))
        return carry

    lax.fori_loop(0, width // LANES, pair_step, 0, unroll=2)


def cross_kernel(
    scale_ref, shift_ref, low_ref, high_ref, ac_ref, inner_ref, mid_ref, w_hbm, wo_hbm,
    mixed_ref, w, wo, keys, values, out0, sems,
):
    width = mid_ref.shape[1]
    copies = []
    for c in range(2):
        cols = slice((c + 1) * width, (c + 2) * width)
        copy = pltpu.make_async_copy(w_hbm.at[:, cols], w.at[c], sems.at[c])
        copy.start()
        copies.append(copy)
    get_wo = pltpu.make_async_copy(wo_hbm, wo, sems.at[2])
    get_wo.start()
    shift = shift_ref[0]
    first = lax.broadcasted_iota(jnp.int32, (WIN, width), 0) < shift
    halo = jnp.where(first, high_ref[...], low_ref[...])
    for c, held in enumerate((keys, values)):
        copies[c].wait()

        def step(n, carry, c=c, held=held):
            cols = pl.ds(pl.multiple_of(n * QUAD, QUAD), QUAD)
            part = dot(halo, w[c, :, cols]).astype(BF16)
            own = ac_ref[c + 1, :, cols]
            early = lax.broadcasted_iota(jnp.int32, part.shape, 0) < shift
            held[:WIN, cols] = jnp.where(early, own, part)
            held[WIN:, cols] = jnp.where(early, part, own)
            return carry

        lax.fori_loop(0, width // QUAD, step, 0)

    def pair_step(pair, carry):
        cols = pl.ds(pl.multiple_of(pair * LANES, LANES), LANES)
        both = dot_t(pair_queries(ac_ref[0, :, cols]), keys[:, cols])
        early = lax.broadcasted_iota(jnp.int32, (2 * WIN, WIN), 0) % WIN < shift
        scores = jnp.where(early, both[:, :WIN], both[:, WIN:])
        probs = soft_rows(scores * pair_scale(scale_ref, pair, scores.shape))
        zero = BF16(0)
        wide = jnp.concatenate(
            [jnp.where(early, probs, zero), jnp.where(early, zero, probs)], axis=1
        )
        part = join_pair(dot(wide, values[:, cols]))
        inner = inner_ref[:, cols]
        early = early[:WIN]
        out0[:WIN, cols] = jnp.where(early, part, inner)
        out0[WIN:, cols] = jnp.where(early, inner, part)
        return carry

    lax.fori_loop(0, width // LANES, pair_step, 0, unroll=2)
    get_wo.wait()

    def out_step(n, carry):
        cols = pl.ds(pl.multiple_of(n * QUAD, QUAD), QUAD)
        total = mid_ref[:, cols].astype(F32) + dot(out0[...], wo[:, cols])
        mixed_ref[:, cols] = total.astype(BF16)
        return carry

    lax.fori_loop(0, width // QUAD, out_step, 0)


VMEM = pl.BlockSpec(memory_space=pltpu.VMEM)
SMEM = pl.BlockSpec(memory_space=pltpu.SMEM)
ANY = pl.BlockSpec(memory_space=pl.ANY)


def call(kernel, out_shape, in_specs, scratch, mib, flops, moved, name):
    return pl.pallas_call(
        kernel,
        out_shape=out_shape,
        in_specs=in_specs,
        out_specs=jax.tree.map(lambda _: VMEM, out_shape),
        scratch_shapes=scratch,
        compiler_params=pltpu.CompilerParams(vmem_limit_bytes=mib * 2**20),
        cost_estimate=pl.CostEstimate(flops=flops, bytes_accessed=moved, transcendentals=0),
        name=name,
    )


def local(
    grid_features,
    mesh_features,
    sources,
    window_shift,
    w_query,
    w_grid_kv,
    w_enc_out,
    norm_gain,
    w_win_qkv,
    w_win_out,
    head_scale,
):
    grid_rows, width = grid_features.shape
    mesh_rows = mesh_features.shape[0]
    edge_count = sources.shape[1]
    heads = head_scale.shape[0]
    lines = width // LANES
    group_edges = RIM * edge_count
    bands = lax.axis_size("band")
    forward = [(i, i + 1) for i in range(bands - 1)]
    backward = [(b, a) for a, b in forward]
    low = lax.ppermute(grid_features[grid_rows - REACH :], "band", forward)
    high = lax.ppermute(grid_features[:REACH], "band", backward)

    rel = (sources - lax.axis_index("band") * grid_rows).reshape(-1)
    own = jnp.clip(rel, 0, grid_rows - 1) * lines
    place = REACH + jnp.arange(group_edges, dtype=jnp.int32)
    rel_low = rel[:group_edges]
    rel_high = rel[-group_edges:]
    rim = jnp.concatenate(
        [
            jnp.where(rel_low < 0, rel_low + REACH, place),
            jnp.where(rel_high >= grid_rows, rel_high - grid_rows, place),
        ]
    ) * lines
    gain = norm_gain.reshape(1, width)

    def arr(*shape, dtype=BF16):
        return jax.ShapeDtypeStruct(shape, dtype)

    full = (mesh_rows, width)
    tile = (WIN, width)
    square = (width, width)
    tiles = pltpu.VMEM((group_edges * lines, LANES), F32)
    edges = pltpu.VMEM((group_edges, width), BF16)
    neg = pltpu.VMEM((heads * RIM, group_edges), F32)
    weight = pltpu.VMEM(square, BF16)
    mid, norm, qrim, xrim = call(
        interior_kernel,
        (
            arr(*full),
            arr(*full),
            arr(2, heads * RIM, width),
            arr(2, group_edges, width),
        ),
        [SMEM, ANY, VMEM, ANY, ANY, ANY, VMEM],
        [
            pltpu.VMEM((grid_rows, width), BF16),
            pltpu.VMEM((grid_rows * lines, LANES), F32),
            pltpu.VMEM((heads, mesh_rows, width), BF16),
            weight, weight, weight, weight,
            pltpu.VMEM(full, BF16),
            tiles, tiles, edges, edges, neg,
            pltpu.VMEM(full, BF16),
            pltpu.SemaphoreType.DMA((4 + grid_rows // 512,)),
        ],
        50, 10**10, 3 * 10**7, "interior",
    )(own, grid_features, mesh_features, w_query, w_grid_kv, w_enc_out, gain)

    table = pltpu.VMEM(((REACH + group_edges) * lines, LANES), F32)
    mid, ac, b = call(
        rim_kernel,
        (arr(*full), arr(*tile), arr(*tile)),
        [SMEM, SMEM, VMEM, VMEM, VMEM, VMEM, VMEM, ANY, ANY, VMEM, VMEM, VMEM],
        [
            table, table, tiles, tiles, edges, edges,
            pltpu.VMEM((heads, 2 * RIM, width), BF16),
            weight, weight, neg,
            pltpu.VMEM((2 * RIM, width), BF16),
            pltpu.SemaphoreType.DMA((2,)),
        ],
        40, 10**9, 10**7, "rims",
    )(rim, window_shift, low, high, qrim, xrim, mesh_features, w_grid_kv, w_enc_out, gain, mid, norm)

    around = forward + [(bands - 1, 0)]
    low_norm = lax.ppermute(ac, "band", around)
    high_norm = lax.ppermute(ac, "band", [(b_, a_) for a_, b_ in around])

    qkv_ac, inner = call(
        inner_kernel,
        (arr(3, *tile), arr(*tile)),
        [SMEM, VMEM, VMEM, ANY],
        [
            pltpu.VMEM((3, *square), BF16),
            pltpu.VMEM((3, *tile), BF16),
            pltpu.SemaphoreType.DMA((3,)),
        ],
        30, 2 * 10**9, 10**7, "inner",
    )(head_scale, ac, b, w_win_qkv)

    return call(
        cross_kernel,
        arr(*full),
        [SMEM, SMEM, VMEM, VMEM, VMEM, VMEM, VMEM, ANY, ANY],
        [
            pltpu.VMEM((2, *square), BF16),
            weight,
            pltpu.VMEM((2 * WIN, width), BF16),
            pltpu.VMEM((2 * WIN, width), BF16),
            pltpu.VMEM(full, BF16),
            pltpu.SemaphoreType.DMA((3,)),
        ],
        30, 2 * 10**9, 10**7, "cross",
    )(head_scale, window_shift, low_norm, high_norm, qkv_ac, inner, mid, w_win_qkv, w_win_out)


def solution(mesh):
    placed = (P("band", None),) * 3 + (P(),) * 8
    return jax.shard_map(
        local, mesh=mesh, in_specs=placed, out_specs=P("band", None), check_vma=False
    )
```

```python
import jax
import jax.numpy as jnp
from jax import lax
from jax.experimental import pallas as pl
from jax.experimental.pallas import tpu as pltpu
from jax.sharding import PartitionSpec as P

WIN = 128
REACH = 384
RIM = 16
HEAD = 64
QUAD = 256
LANES = 128
NEG = -1e30
HALO_FLOPS = 10**10
HALO_BYTES = 3 * 10**7

BF16 = jnp.bfloat16
F32 = jnp.float32


def dot(a, b):
    return jnp.dot(a, b, preferred_element_type=F32)


def dot_t(a, b):
    return lax.dot_general(a, b, (((1,), (1,)), ((), ())), preferred_element_type=F32)


def layer_norm(mid, gain):
    wide = mid.astype(F32)
    center = jnp.mean(wide, axis=-1, keepdims=True)
    spread = jnp.mean((wide - center) ** 2, axis=-1, keepdims=True)
    return ((wide - center) / jnp.sqrt(spread + 1e-05) * gain).astype(BF16)


def count_edges(rel, start, cols):
    nodes, edge_count = rel.shape
    row = lax.broadcasted_iota(jnp.int32, (nodes, cols), 1) + start
    total = jnp.zeros((nodes, cols), F32)
    for e in range(edge_count):
        total += (rel[:, e : e + 1] == row).astype(F32)
    return total


def by_node(values):
    return values.reshape(values.shape[0] // RIM, RIM, values.shape[1])


def masked_scores(queries, rows, count):
    return by_node(dot_t(queries, rows)) + jnp.where(count > 0, 0.0, NEG)[None]


def row_weights(queries, rows, count):
    scores = masked_scores(queries, rows, count)
    top = jnp.max(scores, axis=-1, keepdims=True)
    grown = jnp.exp(scores - top) * count[None]
    weights = grown / jnp.sum(grown, axis=-1, keepdims=True)
    return weights.reshape(queries.shape[0], rows.shape[0]).astype(BF16)


def attend_all(queries, rel, rows_ref, total_ref):
    blocks = rows_ref.shape[0] // WIN
    heads = queries.shape[0] // RIM

    def block(i):
        at = pl.multiple_of(i * WIN, WIN)
        rows = rows_ref[pl.ds(at, WIN), :]
        count = count_edges(rel, at, WIN)
        return rows, count, masked_scores(queries, rows, count)

    def find(i, carry):
        top, size = carry
        _, count, scores = block(i)
        new = jnp.maximum(top, jnp.max(scores, axis=-1, keepdims=True))
        part = jnp.sum(jnp.exp(scores - new) * count[None], axis=-1, keepdims=True)
        return new, size * jnp.exp(top - new) + part

    start = (jnp.full((heads, RIM, 1), NEG, F32), jnp.zeros((heads, RIM, 1), F32))
    top, size = lax.fori_loop(0, blocks, find, start)
    total_ref[...] = jnp.zeros(total_ref.shape, F32)

    def add(i, carry):
        rows, count, scores = block(i)
        weights = jnp.exp(scores - top) * count[None] / size
        total_ref[...] += dot(weights.reshape(heads * RIM, WIN).astype(BF16), rows)
        return carry

    lax.fori_loop(0, blocks, add, 0)
    return total_ref[...].astype(BF16)


def project_heads(pool, w_ref, out_ref, quad):
    per, rows, width = pool.shape
    cols = pl.ds(pl.multiple_of(quad * QUAD, QUAD), QUAD)
    wide = dot(pool.reshape(per * rows, width), w_ref[:, cols])
    head = lax.broadcasted_iota(jnp.int32, (rows, QUAD), 1) // HEAD
    total = wide[:rows]
    for j in range(1, per):
        total = jnp.where(head == j, wide[j * rows : (j + 1) * rows], total)
    out_ref[:, cols] = total.astype(BF16)


def halo_kernel(first_in, last_in, first_ref, last_ref):
    first_ref[...] = first_in[...]
    last_ref[...] = last_in[...]


def interior_kernel(
    rel_ref, x_hbm, mesh_ref, wq_hbm, wkv_hbm, we_hbm, gain_ref,
    mid_ref, norm_ref, qrim_ref,
    x_ref, wq_ref, wkv_ref, we_ref,
    pool, pooled, qs, gathered, total_ref, begin_ref, fits_ref, sems,
):
    width = mesh_ref.shape[1]
    key_cols, value_cols = pl.ds(0, width), pl.ds(width, width)
    copies = [
        pltpu.make_async_copy(source, target, sems.at[i])
        for i, (source, target) in enumerate(
            (
                (wq_hbm, wq_ref),
                (wkv_hbm.at[:, key_cols], wkv_ref.at[:, key_cols]),
                (x_hbm, x_ref),
                (wkv_hbm.at[:, value_cols], wkv_ref.at[:, value_cols]),
                (we_hbm, we_ref),
            )
        )
    ]
    for copy in copies:
        copy.start()
    heads, mesh_rows, width = pool.shape
    grid_rows = x_ref.shape[0]
    quads = width // QUAD
    groups = mesh_rows // RIM
    for group in range(1, groups - 1):
        rel = rel_ref[group * RIM : (group + 1) * RIM, :].astype(F32)
        low = jnp.min(rel).astype(jnp.int32)
        high = jnp.max(rel).astype(jnp.int32)
        begin = jnp.clip(low // 16 * 16, 0, grid_rows - QUAD)
        begin_ref[group] = begin
        fits_ref[group] = (high - begin < QUAD).astype(jnp.int32)
    copies[0].wait()
    for n in range(quads):
        cols = slice(n * QUAD, (n + 1) * QUAD)
        qs[:, cols] = dot(mesh_ref[...], wq_ref[:, cols]).astype(BF16) * BF16(0.125)

    def key_step(t, carry):
        cols = pl.ds(pl.multiple_of(t * QUAD, QUAD), QUAD)
        queries = qs[:, cols]
        head = lax.broadcasted_iota(jnp.int32, queries.shape, 1) // HEAD
        own = jnp.concatenate([jnp.where(head == j, queries, BF16(0)) for j in range(4)], axis=0)
        for n in range(quads):
            some = slice(n * QUAD, (n + 1) * QUAD)
            part = dot_t(own, wkv_ref[some, cols]).astype(BF16)
            pool[pl.ds(t * 4, 4), :, some] = part.reshape(4, mesh_rows, QUAD)
        return carry

    copies[1].wait()
    lax.fori_loop(0, quads, key_step, 0, unroll=4)
    copies[2].wait()
    for side, group in enumerate((0, groups - 1)):
        rows = slice(group * RIM, (group + 1) * RIM)
        qrim_ref[side] = pool[:, rows, :].reshape(heads * RIM, width)
        pooled[:, rows, :] = jnp.zeros((heads, RIM, width), BF16)

    def rows_of(group):
        return pl.ds(pl.multiple_of(group * RIM, RIM), RIM)

    def queries_of(group):
        return pool[:, rows_of(group), :].reshape(heads * RIM, width)

    def put(group, part):
        pooled[:, rows_of(group), :] = part.reshape(heads, RIM, width)

    def group_step(i, carry):
        for k in range(2):
            group = 1 + 2 * i + k
            begin = pl.multiple_of(begin_ref[group], 16)
            rows = x_ref[pl.ds(begin, QUAD), :]
            count = count_edges(rel_ref[rows_of(group), :], begin, QUAD)
            weights = row_weights(queries_of(group), rows, count)
            put(group, dot(weights, rows).astype(BF16))
        return carry

    lax.fori_loop(0, (groups - 2) // 2, group_step, 0, unroll=7)

    def check_step(group, carry):
        @pl.when(fits_ref[group] == 0)
        def _():
            rel = rel_ref[rows_of(group), :]
            put(group, attend_all(queries_of(group), rel, x_ref, total_ref))

        return carry

    lax.fori_loop(1, groups - 1, check_step, 0)

    def value_step(t, carry):
        project_heads(pooled[pl.ds(t * 4, 4)], wkv_ref.at[:, width:], gathered, t)
        return carry

    copies[3].wait()
    lax.fori_loop(0, quads, value_step, 0, unroll=4)
    copies[4].wait()
    for n in range(quads):
        cols = slice(n * QUAD, (n + 1) * QUAD)
        total = mesh_ref[:, cols].astype(F32) + dot(gathered[...], we_ref[:, cols])
        mid_ref[:, cols] = total.astype(BF16)
    norm_ref[...] = layer_norm(mid_ref[...], gain_ref[...])


def rim_kernel(
    rel_ref, shift_ref, low_ref, high_ref, x_hbm, qrim_ref, mesh_ref, wkv_hbm, we_hbm,
    gain_ref, mid_in, norm_in,
    mid_ref, ac_ref, b_ref,
    held_low, held_high, wv_ref, we_ref, pool, gathered, total_ref, sems,
):
    mesh_rows, width = mid_ref.shape
    get_wv = pltpu.make_async_copy(wkv_hbm.at[:, pl.ds(width, width)], wv_ref, sems.at[2])
    get_we = pltpu.make_async_copy(we_hbm, we_ref, sems.at[3])
    grid_rows = x_hbm.shape[0]
    heads = pool.shape[0]
    quads = width // QUAD
    wide = REACH + WIN
    tail = grid_rows - WIN
    near_low = pltpu.make_async_copy(
        x_hbm.at[pl.ds(0, WIN)], held_low.at[pl.ds(REACH, WIN)], sems.at[0]
    )
    near_low.start()
    near_high = pltpu.make_async_copy(
        x_hbm.at[pl.ds(tail, WIN)], held_high.at[pl.ds(tail, WIN)], sems.at[1]
    )
    near_high.start()
    get_wv.start()
    get_we.start()
    held_low[:REACH] = low_ref[...]
    held_high[grid_rows:] = high_ref[...]
    rel_low = rel_ref[:RIM] + REACH
    rel_high = rel_ref[mesh_rows - RIM :]
    count_low = count_edges(rel_low, 0, wide)
    count_high = count_edges(rel_high, tail, wide)
    fits = jnp.max(rel_low.astype(F32)) < wide
    fits_high = jnp.min(rel_high.astype(F32)) >= tail
    near_low.wait()
    near_high.wait()

    def put(side, part):
        pool[:, side * RIM : (side + 1) * RIM, :] = part.reshape(heads, RIM, width)

    weights_low = row_weights(qrim_ref[0], held_low[:wide], count_low)
    weights_high = row_weights(qrim_ref[1], held_high[tail:], count_high)
    put(0, dot(weights_low, held_low[:wide]).astype(BF16))
    put(1, dot(weights_high, held_high[tail:]).astype(BF16))

    @pl.when(jnp.logical_not(jnp.logical_and(fits, fits_high)))
    def _():
        whole_low = pltpu.make_async_copy(x_hbm, held_low.at[pl.ds(REACH, grid_rows)], sems.at[0])
        whole_high = pltpu.make_async_copy(x_hbm, held_high.at[pl.ds(0, grid_rows)], sems.at[1])
        whole_low.start()
        whole_high.start()
        whole_low.wait()
        whole_high.wait()
        put(0, attend_all(qrim_ref[0], rel_low, held_low, total_ref))
        put(1, attend_all(qrim_ref[1], rel_high, held_high, total_ref))

    get_wv.wait()
    for t in range(quads):
        project_heads(pool[t * 4 : (t + 1) * 4], wv_ref, gathered, t)
    get_we.wait()
    edge_mesh = jnp.concatenate([mesh_ref[:RIM], mesh_ref[mesh_rows - RIM :]], axis=0)
    rim_mid = (edge_mesh.astype(F32) + dot(gathered[...], we_ref[...])).astype(BF16)
    rim_norm = layer_norm(rim_mid, gain_ref[...])
    mid_ref[RIM : mesh_rows - RIM] = mid_in[RIM : mesh_rows - RIM]
    mid_ref[:RIM] = rim_mid[:RIM]
    mid_ref[mesh_rows - RIM :] = rim_mid[RIM:]
    tile0 = jnp.concatenate([rim_norm[:RIM], norm_in[RIM:WIN]], axis=0)
    tile1 = jnp.concatenate([norm_in[WIN : mesh_rows - RIM], rim_norm[RIM:]], axis=0)
    first = lax.broadcasted_iota(jnp.int32, tile0.shape, 0) < shift_ref[0]
    ac_ref[...] = jnp.where(first, tile0, tile1)
    b_ref[...] = jnp.where(first, tile1, tile0)


def soft_rows(scores):
    top = jnp.max(scores, axis=-1, keepdims=True)
    grown = jnp.exp(scores - top)
    return (grown / jnp.sum(grown, axis=-1, keepdims=True)).astype(BF16)


def pair_queries(queries):
    second = lax.broadcasted_iota(jnp.int32, queries.shape, 1) >= HEAD
    zero = BF16(0)
    return jnp.concatenate(
        [jnp.where(second, zero, queries), jnp.where(second, queries, zero)], axis=0
    )


def pair_scale(scale_ref, pair, shape):
    upper = lax.broadcasted_iota(jnp.int32, shape, 0) >= shape[0] // 2
    return jnp.where(upper, scale_ref[2 * pair + 1], scale_ref[2 * pair]) * 0.125


def join_pair(wide):
    rows = wide.shape[0] // 2
    second = lax.broadcasted_iota(jnp.int32, (rows, wide.shape[1]), 1) >= HEAD
    return jnp.where(second, wide[rows:], wide[:rows]).astype(BF16)


def inner_kernel(scale_ref, ac_ref, b_ref, w_ref, ac_out, out_ref, qkv):
    width = ac_ref.shape[1]
    rows = jnp.concatenate([ac_ref[...], b_ref[...]], axis=0)
    for n in range(width // QUAD):
        some = slice(n * QUAD, (n + 1) * QUAD)
        for c in range(3):
            at = c * width + n * QUAD
            part = dot(rows, w_ref[:, at : at + QUAD]).astype(BF16)
            ac_out[c, :, some] = part[:WIN]
            qkv[c, :, some] = part[WIN:]
        for pair in range(n * QUAD // LANES, (n + 1) * QUAD // LANES):
            cols = slice(pair * LANES, (pair + 1) * LANES)
            scores = dot_t(pair_queries(qkv[0, :, cols]), qkv[1, :, cols])
            probs = soft_rows(scores * pair_scale(scale_ref, pair, scores.shape))
            out_ref[:, cols] = join_pair(dot(probs, qkv[2, :, cols]))


def cross_kernel(
    scale_ref, shift_ref, low_ref, high_ref, ac_ref, inner_ref, mid_ref, w_ref, wo_ref,
    mixed_ref, keys, values, out0,
):
    width = mid_ref.shape[1]
    shift = shift_ref[0]
    first = lax.broadcasted_iota(jnp.int32, (WIN, width), 0) < shift
    halo = jnp.where(first, high_ref[...], low_ref[...])
    upper = lax.broadcasted_iota(jnp.int32, (WIN, QUAD), 0) < shift
    early = lax.broadcasted_iota(jnp.int32, (2 * WIN, WIN), 0) % WIN < shift
    zero = BF16(0)
    for n in range(width // QUAD):
        some = slice(n * QUAD, (n + 1) * QUAD)
        for c, held in enumerate((keys, values)):
            at = (c + 1) * width + n * QUAD
            part = dot(halo, w_ref[:, at : at + QUAD]).astype(BF16)
            own = ac_ref[c + 1, :, some]
            held[:WIN, some] = jnp.where(upper, own, part)
            held[WIN:, some] = jnp.where(upper, part, own)
        for pair in range(n * QUAD // LANES, (n + 1) * QUAD // LANES):
            cols = slice(pair * LANES, (pair + 1) * LANES)
            both = dot_t(pair_queries(ac_ref[0, :, cols]), keys[:, cols])
            scores = jnp.where(early, both[:, :WIN], both[:, WIN:])
            probs = soft_rows(scores * pair_scale(scale_ref, pair, scores.shape))
            wide = jnp.concatenate(
                [jnp.where(early, probs, zero), jnp.where(early, zero, probs)], axis=1
            )
            part = join_pair(dot(wide, values[:, cols]))
            inner = inner_ref[:, cols]
            out0[:WIN, cols] = jnp.where(early[:WIN], part, inner)
            out0[WIN:, cols] = jnp.where(early[:WIN], inner, part)
    for n in range(width // QUAD):
        some = slice(n * QUAD, (n + 1) * QUAD)
        total = mid_ref[:, some].astype(F32) + dot(out0[...], wo_ref[:, some])
        mixed_ref[:, some] = total.astype(BF16)


VMEM = pl.BlockSpec(memory_space=pltpu.VMEM)
SMEM = pl.BlockSpec(memory_space=pltpu.SMEM)
ANY = pl.BlockSpec(memory_space=pl.ANY)
HBM = pl.BlockSpec(memory_space=pltpu.HBM)


def call(kernel, out_shape, in_specs, scratch, mib, flops, moved, name):
    return pl.pallas_call(
        kernel,
        out_shape=out_shape,
        in_specs=in_specs,
        out_specs=jax.tree.map(lambda _: VMEM, out_shape),
        scratch_shapes=scratch,
        compiler_params=pltpu.CompilerParams(vmem_limit_bytes=mib * 2**20),
        cost_estimate=pl.CostEstimate(flops=flops, bytes_accessed=moved, transcendentals=0),
        name=name,
    )


def local(
    grid_features,
    mesh_features,
    sources,
    window_shift,
    w_query,
    w_grid_kv,
    w_enc_out,
    norm_gain,
    w_win_qkv,
    w_win_out,
    head_scale,
):
    grid_rows, width = grid_features.shape
    mesh_rows = mesh_features.shape[0]
    heads = head_scale.shape[0]
    bands = lax.axis_size("band")
    forward = [(i, i + 1) for i in range(bands - 1)]
    backward = [(b, a) for a, b in forward]
    strip = jax.ShapeDtypeStruct((REACH, width), BF16)
    first_rows, last_rows = call(
        halo_kernel, (strip, strip), [VMEM, VMEM], [], 8, HALO_FLOPS, HALO_BYTES, "halo",
    )(grid_features[:REACH], grid_features[grid_rows - REACH :])
    low = lax.ppermute(last_rows, "band", forward)
    high = lax.ppermute(first_rows, "band", backward)
    rel = sources - lax.axis_index("band") * grid_rows
    gain = norm_gain.reshape(1, width)

    def arr(*shape, dtype=BF16):
        return jax.ShapeDtypeStruct(shape, dtype)

    full = (mesh_rows, width)
    tile = (WIN, width)
    spread = pltpu.VMEM((heads, mesh_rows, width), BF16)
    total = pltpu.VMEM((heads * RIM, width), F32)
    groups = mesh_rows // RIM
    mid, norm, qrim = call(
        interior_kernel,
        (arr(*full), arr(*full), arr(2, heads * RIM, width)),
        [VMEM, HBM, VMEM, HBM, HBM, HBM, VMEM],
        [
            pltpu.VMEM((grid_rows, width), BF16),
            pltpu.VMEM((width, width), BF16),
            pltpu.VMEM((width, 2 * width), BF16),
            pltpu.VMEM((width, width), BF16),
            spread, spread,
            pltpu.VMEM(full, BF16),
            pltpu.VMEM(full, BF16),
            total,
            pltpu.SMEM((groups,), jnp.int32),
            pltpu.SMEM((groups,), jnp.int32),
            pltpu.SemaphoreType.DMA((5,)),
        ],
        52, 10**10, 3 * 10**7, "interior",
    )(rel, grid_features, mesh_features, w_query, w_grid_kv, w_enc_out, gain)

    held = pltpu.VMEM((grid_rows + REACH, width), BF16)
    mid, ac, b = call(
        rim_kernel,
        (arr(*full), arr(*tile), arr(*tile)),
        [VMEM, SMEM, VMEM, VMEM, HBM, VMEM, VMEM, HBM, HBM, VMEM, VMEM, VMEM],
        [
            held, held,
            pltpu.VMEM((width, width), BF16),
            pltpu.VMEM((width, width), BF16),
            pltpu.VMEM((heads, 2 * RIM, width), BF16),
            pltpu.VMEM((2 * RIM, width), BF16),
            total,
            pltpu.SemaphoreType.DMA((4,)),
        ],
        52, 10**9, 10**7, "rims",
    )(
        rel, window_shift, low, high, grid_features, qrim, mesh_features, w_grid_kv, w_enc_out,
        gain, mid, norm,
    )

    around = forward + [(bands - 1, 0)]
    low_norm = lax.ppermute(ac, "band", around)
    high_norm = lax.ppermute(ac, "band", [(b_, a_) for a_, b_ in around])

    qkv_ac, inner = call(
        inner_kernel,
        (arr(3, *tile), arr(*tile)),
        [SMEM, VMEM, VMEM, VMEM],
        [pltpu.VMEM((3, *tile), BF16)],
        16, 2 * 10**9, 10**7, "inner",
    )(head_scale, ac, b, w_win_qkv)

    return call(
        cross_kernel,
        arr(*full),
        [SMEM, SMEM, VMEM, VMEM, VMEM, VMEM, VMEM, VMEM, VMEM],
        [
            pltpu.VMEM((2 * WIN, width), BF16),
            pltpu.VMEM((2 * WIN, width), BF16),
            pltpu.VMEM(full, BF16),
        ],
        16, 2 * 10**9, 10**7, "cross",
    )(head_scale, window_shift, low_norm, high_norm, qkv_ac, inner, mid, w_win_qkv, w_win_out)


def solution(mesh):
    placed = (P("band", None),) * 3 + (P(),) * 8
    return jax.shard_map(
        local, mesh=mesh, in_specs=placed, out_specs=P("band", None), check_vma=False
    )
```

```python
import functools

import jax
import jax.numpy as jnp
from jax import lax
from jax.experimental import pallas as pl
from jax.experimental.pallas import tpu as pltpu
from jax.sharding import PartitionSpec as P

WIN = 128
REACH = 384
RIM = 16
HEAD = 64
QUAD = 256
LANES = 128
NEG = -1e30
HALO_FLOPS = 10**10
HALO_BYTES = 3 * 10**7

BF16 = jnp.bfloat16
F32 = jnp.float32


def dot(a, b):
    return jnp.dot(a, b, preferred_element_type=F32)


def dot_t(a, b):
    return lax.dot_general(a, b, (((1,), (1,)), ((), ())), preferred_element_type=F32)


def layer_norm(mid, gain):
    wide = mid.astype(F32)
    center = jnp.mean(wide, axis=-1, keepdims=True)
    spread = jnp.mean((wide - center) ** 2, axis=-1, keepdims=True)
    return ((wide - center) / jnp.sqrt(spread + 1e-05) * gain).astype(BF16)


def count_edges(rel, start, cols):
    nodes, edge_count = rel.shape
    row = (lax.broadcasted_iota(jnp.int32, (nodes, cols), 1) + start).astype(F32)
    total = jnp.zeros((nodes, cols), F32)
    for e in range(edge_count):
        total += (rel[:, e : e + 1] == row).astype(F32)
    return total


def by_node(values):
    return values.reshape(values.shape[0] // RIM, RIM, values.shape[1])


def masked_scores(queries, rows, count):
    return by_node(dot_t(queries, rows)) + jnp.where(count > 0, 0.0, NEG)[None]


def row_weights(queries, rows, count):
    scores = masked_scores(queries, rows, count)
    top = jnp.max(scores, axis=-1, keepdims=True)
    grown = jnp.exp(scores - top) * count[None]
    weights = grown / jnp.sum(grown, axis=-1, keepdims=True)
    return weights.reshape(queries.shape[0], rows.shape[0]).astype(BF16)


def attend_all(queries, rel, rows_ref, total_ref):
    blocks = rows_ref.shape[0] // WIN
    heads = queries.shape[0] // RIM

    def block(i):
        at = pl.multiple_of(i * WIN, WIN)
        rows = rows_ref[pl.ds(at, WIN), :]
        count = count_edges(rel, at, WIN)
        return rows, count, masked_scores(queries, rows, count)

    def find(i, carry):
        top, size = carry
        _, count, scores = block(i)
        new = jnp.maximum(top, jnp.max(scores, axis=-1, keepdims=True))
        part = jnp.sum(jnp.exp(scores - new) * count[None], axis=-1, keepdims=True)
        return new, size * jnp.exp(top - new) + part

    start = (jnp.full((heads, RIM, 1), NEG, F32), jnp.zeros((heads, RIM, 1), F32))
    top, size = lax.fori_loop(0, blocks, find, start)
    total_ref[...] = jnp.zeros(total_ref.shape, F32)

    def add(i, carry):
        rows, count, scores = block(i)
        weights = jnp.exp(scores - top) * count[None] / size
        total_ref[...] += dot(weights.reshape(heads * RIM, WIN).astype(BF16), rows)
        return carry

    lax.fori_loop(0, blocks, add, 0)
    return total_ref[...].astype(BF16)


def project_heads(pool, w_ref, out_ref, quad):
    per, rows, width = pool.shape
    cols = pl.ds(pl.multiple_of(quad * QUAD, QUAD), QUAD)
    wide = dot(pool.reshape(per * rows, width), w_ref[:, cols])
    head = lax.broadcasted_iota(jnp.int32, (rows, QUAD), 1) // HEAD
    total = wide[:rows]
    for j in range(1, per):
        total = jnp.where(head == j, wide[j * rows : (j + 1) * rows], total)
    out_ref[:, cols] = total.astype(BF16)


def halo_kernel(side_ref, x_hbm, near_ref, far_ref, sems):
    rows = near_ref.shape[0]
    tail = x_hbm.shape[0] - rows
    near_at = jnp.where(side_ref[0] == 0, tail, 0)
    copies = []
    for i, (at, target) in enumerate(((tail - near_at, far_ref), (near_at, near_ref))):
        for k in range(rows // WIN):
            place = pl.ds(pl.multiple_of(at + k * WIN, WIN), WIN)
            sem = sems.at[i * (rows // WIN) + k]
            target_rows = target.at[pl.ds(k * WIN, WIN)]
            copies.append(pltpu.make_async_copy(x_hbm.at[place], target_rows, sem))
    for copy in copies:
        copy.start()
    for copy in copies:
        copy.wait()


def interior_kernel(
    edge_count, shift_ref, edge_ref, x_hbm, mesh_ref, wq_hbm, wkv_hbm, we_hbm, gain_ref,
    mid_ref, ac_ref, b_ref, qrim_ref,
    x_ref, wq_ref, wkv_ref, we_ref,
    rel_ref, pool, pooled, qs, gathered, total_ref, begin_ref, fits_ref, sems,
):
    width = mesh_ref.shape[1]
    key_cols, value_cols = pl.ds(0, width), pl.ds(width, width)
    copies = [
        pltpu.make_async_copy(source, target, sems.at[i])
        for i, (source, target) in enumerate(
            (
                (wq_hbm, wq_ref),
                (wkv_hbm.at[:, key_cols], wkv_ref.at[:, key_cols]),
                (x_hbm, x_ref),
                (wkv_hbm.at[:, value_cols], wkv_ref.at[:, value_cols]),
                (we_hbm, we_ref),
            )
        )
    ]
    for copy in copies:
        copy.start()
    heads, mesh_rows, width = pool.shape
    grid_rows = x_ref.shape[0]
    quads = width // QUAD
    groups = mesh_rows // RIM
    rel_ref[...] = edge_ref[...].astype(F32).T
    for group in range(1, groups - 1):
        rel = rel_ref[group * RIM : (group + 1) * RIM, :edge_count]
        low = jnp.min(rel).astype(jnp.int32)
        high = jnp.max(rel).astype(jnp.int32)
        begin = jnp.clip(low // 16 * 16, 0, grid_rows - QUAD)
        begin_ref[group] = begin
        fits_ref[group] = (high - begin < QUAD).astype(jnp.int32)
    copies[0].wait()
    for n in range(quads):
        cols = slice(n * QUAD, (n + 1) * QUAD)
        qs[:, cols] = dot(mesh_ref[...], wq_ref[:, cols]).astype(BF16) * BF16(0.125)

    def key_step(t, carry):
        cols = pl.ds(pl.multiple_of(t * QUAD, QUAD), QUAD)
        queries = qs[:, cols]
        head = lax.broadcasted_iota(jnp.int32, queries.shape, 1) // HEAD
        own = jnp.concatenate([jnp.where(head == j, queries, BF16(0)) for j in range(4)], axis=0)
        for n in range(quads):
            some = slice(n * QUAD, (n + 1) * QUAD)
            part = dot_t(own, wkv_ref[some, cols]).astype(BF16)
            pool[pl.ds(t * 4, 4), :, some] = part.reshape(4, mesh_rows, QUAD)
        return carry

    copies[1].wait()
    lax.fori_loop(0, quads, key_step, 0, unroll=4)
    copies[2].wait()
    for side, group in enumerate((0, groups - 1)):
        rows = slice(group * RIM, (group + 1) * RIM)
        qrim_ref[side] = pool[:, rows, :].reshape(heads * RIM, width)
        pooled[:, rows, :] = jnp.zeros((heads, RIM, width), BF16)

    def rows_of(group):
        return pl.ds(pl.multiple_of(group * RIM, RIM), RIM)

    def queries_of(group):
        return pool[:, rows_of(group), :].reshape(heads * RIM, width)

    def put(group, part):
        pooled[:, rows_of(group), :] = part.reshape(heads, RIM, width)

    def group_step(i, carry):
        for k in range(2):
            group = 1 + 2 * i + k
            begin = pl.multiple_of(begin_ref[group], 16)
            rows = x_ref[pl.ds(begin, QUAD), :]
            count = count_edges(rel_ref[rows_of(group), :edge_count], begin, QUAD)
            weights = row_weights(queries_of(group), rows, count)
            put(group, dot(weights, rows).astype(BF16))
        return carry

    lax.fori_loop(0, (groups - 2) // 2, group_step, 0, unroll=7)

    def check_step(group, carry):
        @pl.when(fits_ref[group] == 0)
        def _():
            rel = rel_ref[rows_of(group), :edge_count]
            put(group, attend_all(queries_of(group), rel, x_ref, total_ref))

        return carry

    lax.fori_loop(1, groups - 1, check_step, 0)

    def value_step(t, carry):
        project_heads(pooled[pl.ds(t * 4, 4)], wkv_ref.at[:, width:], gathered, t)
        return carry

    copies[3].wait()
    lax.fori_loop(0, quads, value_step, 0, unroll=4)
    copies[4].wait()
    for n in range(quads):
        cols = slice(n * QUAD, (n + 1) * QUAD)
        total = mesh_ref[:, cols].astype(F32) + dot(gathered[...], we_ref[:, cols])
        mid_ref[:, cols] = total.astype(BF16)
    norm = layer_norm(mid_ref[...], gain_ref[...])
    first = lax.broadcasted_iota(jnp.int32, (WIN, width), 0) < shift_ref[0]
    ac_ref[...] = jnp.where(first, norm[:WIN], norm[WIN:])
    b_ref[...] = jnp.where(first, norm[WIN:], norm[:WIN])


def rim_kernel(
    edge_count, side_ref, shift_ref, edge_ref, near_ref, far_ref, x_hbm, qrim_ref, mesh_ref, wkv_hbm, we_hbm,
    gain_ref, mid_in, ac_in, b_in,
    mid_ref, ac_ref, b_ref,
    held_low, held_high, wv_ref, we_ref, pool, gathered, total_ref, sems,
):
    mesh_rows, width = mid_ref.shape
    get_wv = pltpu.make_async_copy(wkv_hbm.at[:, pl.ds(width, width)], wv_ref, sems.at[2])
    get_we = pltpu.make_async_copy(we_hbm, we_ref, sems.at[3])
    grid_rows = x_hbm.shape[0]
    heads = pool.shape[0]
    quads = width // QUAD
    wide = REACH + WIN
    tail = grid_rows - WIN
    near_low = pltpu.make_async_copy(
        x_hbm.at[pl.ds(0, WIN)], held_low.at[pl.ds(REACH, WIN)], sems.at[0]
    )
    near_low.start()
    near_high = pltpu.make_async_copy(
        x_hbm.at[pl.ds(tail, WIN)], held_high.at[pl.ds(tail, WIN)], sems.at[1]
    )
    near_high.start()
    get_wv.start()
    get_we.start()
    even = side_ref[0] == 0

    @pl.when(even)
    def _():
        held_low[:REACH] = far_ref[...]
        held_high[grid_rows:] = near_ref[...]

    @pl.when(jnp.logical_not(even))
    def _():
        held_low[:REACH] = near_ref[...]
        held_high[grid_rows:] = far_ref[...]

    rel = edge_ref[...].astype(F32).T
    rel_low = rel[:RIM, :edge_count] + float(REACH)
    rel_high = rel[mesh_rows - RIM :, :edge_count]
    count_low = count_edges(rel_low, 0, wide)
    count_high = count_edges(rel_high, tail, wide)
    fits = jnp.max(rel_low) < wide
    fits_high = jnp.min(rel_high) >= tail
    near_low.wait()
    near_high.wait()

    def put(side, part):
        pool[:, side * RIM : (side + 1) * RIM, :] = part.reshape(heads, RIM, width)

    weights_low = row_weights(qrim_ref[0], held_low[:wide], count_low)
    weights_high = row_weights(qrim_ref[1], held_high[tail:], count_high)
    put(0, dot(weights_low, held_low[:wide]).astype(BF16))
    put(1, dot(weights_high, held_high[tail:]).astype(BF16))

    @pl.when(jnp.logical_not(jnp.logical_and(fits, fits_high)))
    def _():
        whole_low = pltpu.make_async_copy(x_hbm, held_low.at[pl.ds(REACH, grid_rows)], sems.at[0])
        whole_high = pltpu.make_async_copy(x_hbm, held_high.at[pl.ds(0, grid_rows)], sems.at[1])
        whole_low.start()
        whole_high.start()
        whole_low.wait()
        whole_high.wait()
        put(0, attend_all(qrim_ref[0], rel_low, held_low, total_ref))
        put(1, attend_all(qrim_ref[1], rel_high, held_high, total_ref))

    get_wv.wait()
    for t in range(quads):
        project_heads(pool[t * 4 : (t + 1) * 4], wv_ref, gathered, t)
    get_we.wait()
    edge_mesh = jnp.concatenate([mesh_ref[:RIM], mesh_ref[mesh_rows - RIM :]], axis=0)
    rim_mid = (edge_mesh.astype(F32) + dot(gathered[...], we_ref[...])).astype(BF16)
    rim_norm = layer_norm(rim_mid, gain_ref[...])
    row = lax.broadcasted_iota(jnp.int32, (RIM, width), 0)
    for side in range(2):
        part = slice(side * RIM, (side + 1) * RIM)
        at = slice(side * (mesh_rows - RIM), side * (mesh_rows - RIM) + RIM)
        mid_ref[at] = rim_mid[part]
        at = slice(side * (WIN - RIM), side * (WIN - RIM) + RIM)
        crosses = (row + at.start < shift_ref[0]).astype(jnp.int32) != side
        ac_ref[at] = jnp.where(crosses, rim_norm[part], ac_in[at])
        b_ref[at] = jnp.where(crosses, b_in[at], rim_norm[part])


def soft_rows(scores):
    top = jnp.max(scores, axis=-1, keepdims=True)
    grown = jnp.exp(scores - top)
    return (grown / jnp.sum(grown, axis=-1, keepdims=True)).astype(BF16)


def pair_queries(queries):
    second = lax.broadcasted_iota(jnp.int32, queries.shape, 1) >= HEAD
    zero = BF16(0)
    return jnp.concatenate(
        [jnp.where(second, zero, queries), jnp.where(second, queries, zero)], axis=0
    )


def pair_scale(scale_ref, pair, shape):
    upper = lax.broadcasted_iota(jnp.int32, shape, 0) >= shape[0] // 2
    return jnp.where(upper, scale_ref[2 * pair + 1], scale_ref[2 * pair]) * 0.125


def join_pair(wide):
    rows = wide.shape[0] // 2
    second = lax.broadcasted_iota(jnp.int32, (rows, wide.shape[1]), 1) >= HEAD
    return jnp.where(second, wide[rows:], wide[:rows]).astype(BF16)


def inner_kernel(scale_ref, ac_ref, b_ref, w_ref, ac_out, out_ref, qkv):
    width = ac_ref.shape[1]
    rows = jnp.concatenate([ac_ref[...], b_ref[...]], axis=0)
    for n in range(width // QUAD):
        some = slice(n * QUAD, (n + 1) * QUAD)
        for c in range(3):
            at = c * width + n * QUAD
            part = dot(rows, w_ref[:, at : at + QUAD]).astype(BF16)
            ac_out[c, :, some] = part[:WIN]
            qkv[c, :, some] = part[WIN:]
        for pair in range(n * QUAD // LANES, (n + 1) * QUAD // LANES):
            cols = slice(pair * LANES, (pair + 1) * LANES)
            scores = dot_t(pair_queries(qkv[0, :, cols]), qkv[1, :, cols])
            probs = soft_rows(scores * pair_scale(scale_ref, pair, scores.shape))
            out_ref[:, cols] = join_pair(dot(probs, qkv[2, :, cols]))


def cross_kernel(
    scale_ref, side_ref, shift_ref, near_ref, far_ref, ac_ref, inner_ref, mid_ref, w_ref, wo_ref,
    mixed_ref, keys, values, out0,
):
    width = mid_ref.shape[1]
    shift = shift_ref[0]
    first = (lax.broadcasted_iota(jnp.int32, (WIN, width), 0) < shift).astype(jnp.int32)
    halo = jnp.where(first != side_ref[0], near_ref[...], far_ref[...])
    upper = lax.broadcasted_iota(jnp.int32, (WIN, QUAD), 0) < shift
    early = lax.broadcasted_iota(jnp.int32, (2 * WIN, WIN), 0) % WIN < shift
    zero = BF16(0)
    for n in range(width // QUAD):
        some = slice(n * QUAD, (n + 1) * QUAD)
        for c, held in enumerate((keys, values)):
            at = (c + 1) * width + n * QUAD
            part = dot(halo, w_ref[:, at : at + QUAD]).astype(BF16)
            own = ac_ref[c + 1, :, some]
            held[:WIN, some] = jnp.where(upper, own, part)
            held[WIN:, some] = jnp.where(upper, part, own)
        for pair in range(n * QUAD // LANES, (n + 1) * QUAD // LANES):
            cols = slice(pair * LANES, (pair + 1) * LANES)
            both = dot_t(pair_queries(ac_ref[0, :, cols]), keys[:, cols])
            scores = jnp.where(early, both[:, :WIN], both[:, WIN:])
            probs = soft_rows(scores * pair_scale(scale_ref, pair, scores.shape))
            wide = jnp.concatenate(
                [jnp.where(early, probs, zero), jnp.where(early, zero, probs)], axis=1
            )
            part = join_pair(dot(wide, values[:, cols]))
            inner = inner_ref[:, cols]
            out0[:WIN, cols] = jnp.where(early[:WIN], part, inner)
            out0[WIN:, cols] = jnp.where(early[:WIN], inner, part)
    for n in range(width // QUAD):
        some = slice(n * QUAD, (n + 1) * QUAD)
        total = mid_ref[:, some].astype(F32) + dot(out0[...], wo_ref[:, some])
        mixed_ref[:, some] = total.astype(BF16)


VMEM = pl.BlockSpec(memory_space=pltpu.VMEM)
SMEM = pl.BlockSpec(memory_space=pltpu.SMEM)
ANY = pl.BlockSpec(memory_space=pl.ANY)
HBM = pl.BlockSpec(memory_space=pltpu.HBM)


def call(kernel, out_shape, in_specs, scratch, mib, flops, moved, name, aliases={}):
    return pl.pallas_call(
        kernel,
        out_shape=out_shape,
        in_specs=in_specs,
        out_specs=jax.tree.map(lambda _: VMEM, out_shape),
        scratch_shapes=scratch,
        input_output_aliases=aliases,
        compiler_params=pltpu.CompilerParams(vmem_limit_bytes=mib * 2**20),
        cost_estimate=pl.CostEstimate(flops=flops, bytes_accessed=moved, transcendentals=0),
        name=name,
    )


def local(
    grid_features,
    mesh_features,
    sources,
    window_shift,
    w_query,
    w_grid_kv,
    w_enc_out,
    norm_gain,
    w_win_qkv,
    w_win_out,
    head_scale,
):
    grid_rows, width = grid_features.shape
    mesh_rows = mesh_features.shape[0]
    heads = head_scale.shape[0]
    edge_count = sources.shape[1]
    bands = lax.axis_size("band")
    band = lax.axis_index("band")
    side = (band % 2).astype(jnp.int32).reshape(1)
    near = [(i, i ^ 1) for i in range(bands)]
    far = [pair for i in range(1, bands - 1, 2) for pair in ((i, i + 1), (i + 1, i))]
    around = far + [(bands - 1, 0), (0, bands - 1)]
    strip = jax.ShapeDtypeStruct((REACH, width), BF16)
    near_rows, far_rows = call(
        halo_kernel, (strip, strip), [SMEM, HBM],
        [pltpu.SemaphoreType.DMA((2 * REACH // WIN,))], 57, HALO_FLOPS, HALO_BYTES, "halo",
    )(side, grid_features)
    far_grid = lax.ppermute(far_rows, "band", far)
    near_grid = lax.ppermute(near_rows, "band", near)
    rel = jnp.pad(sources.T - band * grid_rows, ((0, -edge_count % 8), (0, 0)))
    gain = norm_gain.reshape(1, width)

    def arr(*shape, dtype=BF16):
        return jax.ShapeDtypeStruct(shape, dtype)

    full = (mesh_rows, width)
    tile = (WIN, width)
    spread = pltpu.VMEM((heads, mesh_rows, width), BF16)
    total = pltpu.VMEM((heads * RIM, width), F32)
    groups = mesh_rows // RIM
    mid, ac, b, qrim = call(
        functools.partial(interior_kernel, edge_count),
        (arr(*full), arr(*tile), arr(*tile), arr(2, heads * RIM, width)),
        [SMEM, VMEM, HBM, VMEM, HBM, HBM, HBM, VMEM],
        [
            pltpu.VMEM((grid_rows, width), BF16),
            pltpu.VMEM((width, width), BF16),
            pltpu.VMEM((width, 2 * width), BF16),
            pltpu.VMEM((width, width), BF16),
            pltpu.VMEM((mesh_rows, rel.shape[0]), F32),
            spread, spread,
            pltpu.VMEM(full, BF16),
            pltpu.VMEM(full, BF16),
            total,
            pltpu.SMEM((groups,), jnp.int32),
            pltpu.SMEM((groups,), jnp.int32),
            pltpu.SemaphoreType.DMA((5,)),
        ],
        52, 10**10, 3 * 10**7, "interior",
    )(window_shift, rel, grid_features, mesh_features, w_query, w_grid_kv, w_enc_out, gain)

    held = pltpu.VMEM((grid_rows + REACH, width), BF16)
    mid, ac, b = call(
        functools.partial(rim_kernel, edge_count),
        (arr(*full), arr(*tile), arr(*tile)),
        [SMEM, SMEM, VMEM, VMEM, VMEM, HBM, VMEM, VMEM, HBM, HBM] + [VMEM] * 4,
        [
            held, held,
            pltpu.VMEM((width, width), BF16),
            pltpu.VMEM((width, width), BF16),
            pltpu.VMEM((heads, 2 * RIM, width), BF16),
            pltpu.VMEM((2 * RIM, width), BF16),
            total,
            pltpu.SemaphoreType.DMA((4,)),
        ],
        50, 10**9, 10**7, "rims", {11: 0, 12: 1, 13: 2},
    )(
        side, window_shift, rel, near_grid, far_grid, grid_features, qrim, mesh_features,
        w_grid_kv, w_enc_out, gain, mid, ac, b,
    )

    far_norm = lax.ppermute(ac, "band", around)
    near_norm = lax.ppermute(ac, "band", near)

    qkv_ac, inner = call(
        inner_kernel,
        (arr(3, *tile), arr(*tile)),
        [SMEM, VMEM, VMEM, VMEM],
        [pltpu.VMEM((3, *tile), BF16)],
        16, 2 * 10**9, 10**7, "inner",
    )(head_scale, ac, b, w_win_qkv)

    return call(
        cross_kernel,
        arr(*full),
        [SMEM] * 3 + [VMEM] * 7,
        [
            pltpu.VMEM((2 * WIN, width), BF16),
            pltpu.VMEM((2 * WIN, width), BF16),
            pltpu.VMEM(full, BF16),
        ],
        16, 2 * 10**9, 10**7, "cross",
    )(head_scale, side, window_shift, near_norm, far_norm, qkv_ac, inner, mid, w_win_qkv, w_win_out)


def solution(mesh):
    placed = (P("band", None),) * 3 + (P(),) * 8
    return jax.shard_map(
        local, mesh=mesh, in_specs=placed, out_specs=P("band", None), check_vma=False
    )
```

```python
import functools

import jax
import jax.numpy as jnp
from jax import lax
from jax.experimental import pallas as pl
from jax.experimental.pallas import tpu as pltpu
from jax.sharding import PartitionSpec as P

WIN = 128
REACH = 384
RIM = 16
HEAD = 64
QUAD = 256
LANES = 128
NEG = -1e30
HALO_FLOPS = 10**10
HALO_BYTES = 3 * 10**7

BF16 = jnp.bfloat16
F32 = jnp.float32


def dot(a, b):
    return jnp.dot(a, b, preferred_element_type=F32)


def dot_t(a, b):
    return lax.dot_general(a, b, (((1,), (1,)), ((), ())), preferred_element_type=F32)


def layer_norm(mid, gain):
    wide = mid.astype(F32)
    center = jnp.mean(wide, axis=-1, keepdims=True)
    spread = jnp.mean((wide - center) ** 2, axis=-1, keepdims=True)
    return ((wide - center) / jnp.sqrt(spread + 1e-05) * gain).astype(BF16)


def count_edges(rel, start, cols):
    nodes, edge_count = rel.shape
    row = (lax.broadcasted_iota(jnp.int32, (nodes, cols), 1) + start).astype(F32)
    total = jnp.zeros((nodes, cols), F32)
    for e in range(edge_count):
        total += (rel[:, e : e + 1] == row).astype(F32)
    return total


def by_node(values):
    return values.reshape(values.shape[0] // RIM, RIM, values.shape[1])


def masked_scores(queries, rows, count):
    return by_node(dot_t(queries, rows)) + jnp.where(count > 0, 0.0, NEG)[None]


def row_weights(queries, rows, count):
    scores = masked_scores(queries, rows, count)
    top = jnp.max(scores, axis=-1, keepdims=True)
    grown = jnp.exp(scores - top) * count[None]
    weights = grown / jnp.sum(grown, axis=-1, keepdims=True)
    return weights.reshape(queries.shape[0], rows.shape[0]).astype(BF16)


def attend_all(queries, rel, rows_ref, total_ref):
    blocks = rows_ref.shape[0] // WIN
    heads = queries.shape[0] // RIM

    def block(i):
        at = pl.multiple_of(i * WIN, WIN)
        rows = rows_ref[pl.ds(at, WIN), :]
        count = count_edges(rel, at, WIN)
        return rows, count, masked_scores(queries, rows, count)

    def find(i, carry):
        top, size = carry
        _, count, scores = block(i)
        new = jnp.maximum(top, jnp.max(scores, axis=-1, keepdims=True))
        part = jnp.sum(jnp.exp(scores - new) * count[None], axis=-1, keepdims=True)
        return new, size * jnp.exp(top - new) + part

    start = (jnp.full((heads, RIM, 1), NEG, F32), jnp.zeros((heads, RIM, 1), F32))
    top, size = lax.fori_loop(0, blocks, find, start)
    total_ref[...] = jnp.zeros(total_ref.shape, F32)

    def add(i, carry):
        rows, count, scores = block(i)
        weights = jnp.exp(scores - top) * count[None] / size
        total_ref[...] += dot(weights.reshape(heads * RIM, WIN).astype(BF16), rows)
        return carry

    lax.fori_loop(0, blocks, add, 0)
    return total_ref[...].astype(BF16)


def project_heads(pool, w_ref, out_ref, quad):
    per, rows, width = pool.shape
    cols = pl.ds(pl.multiple_of(quad * QUAD, QUAD), QUAD)
    wide = dot(pool.reshape(per * rows, width), w_ref[:, cols])
    head = lax.broadcasted_iota(jnp.int32, (rows, QUAD), 1) // HEAD
    total = wide[:rows]
    for j in range(1, per):
        total = jnp.where(head == j, wide[j * rows : (j + 1) * rows], total)
    out_ref[:, cols] = total.astype(BF16)


def halo_kernel(side_ref, x_hbm, near_hbm, far_hbm, held, in_sems, out_sems):
    rows = near_hbm.shape[0]
    tail = x_hbm.shape[0] - rows
    near_at = jnp.where(side_ref[0] == 0, tail, 0)
    fetches, sends = [], []
    for i, (at, target) in enumerate(((tail - near_at, far_hbm), (near_at, near_hbm))):
        for k in range(rows // WIN):
            n = i * (rows // WIN) + k
            place = pl.ds(pl.multiple_of(at + k * WIN, WIN), WIN)
            target_rows = target.at[pl.ds(k * WIN, WIN)]
            fetches.append(pltpu.make_async_copy(x_hbm.at[place], held.at[n], in_sems.at[n]))
            sends.append(pltpu.make_async_copy(held.at[n], target_rows, out_sems.at[n]))
    for fetch in fetches:
        fetch.start()
    for fetch, send in zip(fetches, sends):
        fetch.wait()
        send.start()
    for send in sends:
        send.wait()


def interior_kernel(
    edge_count, shift_ref, edge_ref, x_hbm, mesh_ref, wq_hbm, wkv_hbm, we_hbm, gain_ref,
    mid_ref, ac_ref, b_ref, qrim_ref,
    x_ref, wq_ref, wkv_ref, we_ref,
    rel_ref, pool, pooled, qs, gathered, total_ref, begin_ref, fits_ref, sems,
):
    width = mesh_ref.shape[1]
    key_cols, value_cols = pl.ds(0, width), pl.ds(width, width)
    copies = [
        pltpu.make_async_copy(source, target, sems.at[i])
        for i, (source, target) in enumerate(
            (
                (wq_hbm, wq_ref),
                (wkv_hbm.at[:, key_cols], wkv_ref.at[:, key_cols]),
                (x_hbm, x_ref),
                (wkv_hbm.at[:, value_cols], wkv_ref.at[:, value_cols]),
                (we_hbm, we_ref),
            )
        )
    ]
    for copy in copies:
        copy.start()
    heads, mesh_rows, width = pool.shape
    grid_rows = x_ref.shape[0]
    quads = width // QUAD
    groups = mesh_rows // RIM
    rel_ref[...] = edge_ref[...].astype(F32).T
    for group in range(1, groups - 1):
        rel = rel_ref[group * RIM : (group + 1) * RIM, :edge_count]
        low = jnp.min(rel).astype(jnp.int32)
        high = jnp.max(rel).astype(jnp.int32)
        begin = jnp.clip(low // 16 * 16, 0, grid_rows - QUAD)
        begin_ref[group] = begin
        fits_ref[group] = (high - begin < QUAD).astype(jnp.int32)
    copies[0].wait()
    for n in range(quads):
        cols = slice(n * QUAD, (n + 1) * QUAD)
        qs[:, cols] = dot(mesh_ref[...], wq_ref[:, cols]).astype(BF16) * BF16(0.125)

    def key_step(t, carry):
        cols = pl.ds(pl.multiple_of(t * QUAD, QUAD), QUAD)
        queries = qs[:, cols]
        head = lax.broadcasted_iota(jnp.int32, queries.shape, 1) // HEAD
        own = jnp.concatenate([jnp.where(head == j, queries, BF16(0)) for j in range(4)], axis=0)
        for n in range(quads):
            some = slice(n * QUAD, (n + 1) * QUAD)
            part = dot_t(own, wkv_ref[some, cols]).astype(BF16)
            pool[pl.ds(t * 4, 4), :, some] = part.reshape(4, mesh_rows, QUAD)
        return carry

    copies[1].wait()
    lax.fori_loop(0, quads, key_step, 0, unroll=4)
    copies[2].wait()
    for side, group in enumerate((0, groups - 1)):
        rows = slice(group * RIM, (group + 1) * RIM)
        qrim_ref[side] = pool[:, rows, :].reshape(heads * RIM, width)
        pooled[:, rows, :] = jnp.zeros((heads, RIM, width), BF16)

    def rows_of(group):
        return pl.ds(pl.multiple_of(group * RIM, RIM), RIM)

    def queries_of(group):
        return pool[:, rows_of(group), :].reshape(heads * RIM, width)

    def put(group, part):
        pooled[:, rows_of(group), :] = part.reshape(heads, RIM, width)

    def group_step(i, carry):
        for k in range(2):
            group = 1 + 2 * i + k
            begin = pl.multiple_of(begin_ref[group], 16)
            rows = x_ref[pl.ds(begin, QUAD), :]
            count = count_edges(rel_ref[rows_of(group), :edge_count], begin, QUAD)
            weights = row_weights(queries_of(group), rows, count)
            put(group, dot(weights, rows).astype(BF16))
        return carry

    lax.fori_loop(0, (groups - 2) // 2, group_step, 0, unroll=7)

    def check_step(group, carry):
        @pl.when(fits_ref[group] == 0)
        def _():
            rel = rel_ref[rows_of(group), :edge_count]
            put(group, attend_all(queries_of(group), rel, x_ref, total_ref))

        return carry

    lax.fori_loop(1, groups - 1, check_step, 0)

    def value_step(t, carry):
        project_heads(pooled[pl.ds(t * 4, 4)], wkv_ref.at[:, width:], gathered, t)
        return carry

    copies[3].wait()
    lax.fori_loop(0, quads, value_step, 0, unroll=4)
    copies[4].wait()
    for n in range(quads):
        cols = slice(n * QUAD, (n + 1) * QUAD)
        total = mesh_ref[:, cols].astype(F32) + dot(gathered[...], we_ref[:, cols])
        mid_ref[:, cols] = total.astype(BF16)
    norm = layer_norm(mid_ref[...], gain_ref[...])
    first = lax.broadcasted_iota(jnp.int32, (WIN, width), 0) < shift_ref[0]
    ac_ref[...] = jnp.where(first, norm[:WIN], norm[WIN:])
    b_ref[...] = jnp.where(first, norm[WIN:], norm[:WIN])


def rim_kernel(
    edge_count, side_ref, shift_ref, edge_ref, near_hbm, far_hbm, x_hbm, qrim_hbm, mesh_ref, wkv_hbm, we_hbm,
    gain_ref, mid_in, ac_in, b_in,
    mid_ref, ac_ref, b_ref,
    held, qrim_ref, wv_ref, we_ref, pool, gathered, total_ref, sems,
):
    mesh_rows, width = mid_ref.shape
    get_wv = pltpu.make_async_copy(wkv_hbm.at[:, pl.ds(width, width)], wv_ref, sems.at[5])
    get_we = pltpu.make_async_copy(we_hbm, we_ref, sems.at[6])
    grid_rows = x_hbm.shape[0]
    heads = pool.shape[0]
    quads = width // QUAD
    wide = REACH + WIN
    tail = grid_rows - WIN
    held_low, held_high = held.at[0], held.at[1]
    side = side_ref[0]
    copies = [
        pltpu.make_async_copy(qrim_hbm, qrim_ref, sems.at[0]),
        pltpu.make_async_copy(
            x_hbm.at[pl.ds(0, WIN)], held_low.at[pl.ds(REACH, WIN)], sems.at[1]
        ),
        pltpu.make_async_copy(
            x_hbm.at[pl.ds(tail, WIN)], held_high.at[pl.ds(tail, WIN)], sems.at[2]
        ),
    ]
    for i, (end, source) in enumerate(((side, far_hbm), (1 - side, near_hbm))):
        rows = pl.ds(pl.multiple_of(end * grid_rows, WIN), REACH)
        copies.append(pltpu.make_async_copy(source, held.at[end, rows], sems.at[3 + i]))
    for copy in copies:
        copy.start()
    get_wv.start()
    get_we.start()
    rel = edge_ref[...].astype(F32).T
    rel_low = rel[:RIM, :edge_count] + float(REACH)
    rel_high = rel[mesh_rows - RIM :, :edge_count]
    count_low = count_edges(rel_low, 0, wide)
    count_high = count_edges(rel_high, tail, wide)
    fits = jnp.max(rel_low) < wide
    fits_high = jnp.min(rel_high) >= tail
    for copy in copies:
        copy.wait()

    def put(side, part):
        pool[:, side * RIM : (side + 1) * RIM, :] = part.reshape(heads, RIM, width)

    weights_low = row_weights(qrim_ref[0], held_low[:wide], count_low)
    weights_high = row_weights(qrim_ref[1], held_high[tail:], count_high)
    put(0, dot(weights_low, held_low[:wide]).astype(BF16))
    put(1, dot(weights_high, held_high[tail:]).astype(BF16))

    @pl.when(jnp.logical_not(jnp.logical_and(fits, fits_high)))
    def _():
        whole_low = pltpu.make_async_copy(x_hbm, held_low.at[pl.ds(REACH, grid_rows)], sems.at[0])
        whole_high = pltpu.make_async_copy(x_hbm, held_high.at[pl.ds(0, grid_rows)], sems.at[1])
        whole_low.start()
        whole_high.start()
        whole_low.wait()
        whole_high.wait()
        put(0, attend_all(qrim_ref[0], rel_low, held_low, total_ref))
        put(1, attend_all(qrim_ref[1], rel_high, held_high, total_ref))

    get_wv.wait()
    for t in range(quads):
        project_heads(pool[t * 4 : (t + 1) * 4], wv_ref, gathered, t)
    get_we.wait()
    edge_mesh = jnp.concatenate([mesh_ref[:RIM], mesh_ref[mesh_rows - RIM :]], axis=0)
    rim_mid = (edge_mesh.astype(F32) + dot(gathered[...], we_ref[...])).astype(BF16)
    rim_norm = layer_norm(rim_mid, gain_ref[...])
    inside = slice(RIM, mesh_rows - RIM)
    mid_ref[inside] = mid_in[inside]
    inside = slice(RIM, WIN - RIM)
    ac_ref[inside] = ac_in[inside]
    b_ref[inside] = b_in[inside]
    row = lax.broadcasted_iota(jnp.int32, (RIM, width), 0)
    for side in range(2):
        part = slice(side * RIM, (side + 1) * RIM)
        at = slice(side * (mesh_rows - RIM), side * (mesh_rows - RIM) + RIM)
        mid_ref[at] = rim_mid[part]
        at = slice(side * (WIN - RIM), side * (WIN - RIM) + RIM)
        crosses = (row + at.start < shift_ref[0]).astype(jnp.int32) != side
        ac_ref[at] = jnp.where(crosses, rim_norm[part], ac_in[at])
        b_ref[at] = jnp.where(crosses, b_in[at], rim_norm[part])


def soft_rows(scores):
    top = jnp.max(scores, axis=-1, keepdims=True)
    grown = jnp.exp(scores - top)
    return (grown / jnp.sum(grown, axis=-1, keepdims=True)).astype(BF16)


def pair_queries(queries):
    second = lax.broadcasted_iota(jnp.int32, queries.shape, 1) >= HEAD
    zero = BF16(0)
    return jnp.concatenate(
        [jnp.where(second, zero, queries), jnp.where(second, queries, zero)], axis=0
    )


def pair_scale(scale_ref, pair, shape):
    upper = lax.broadcasted_iota(jnp.int32, shape, 0) >= shape[0] // 2
    return jnp.where(upper, scale_ref[2 * pair + 1], scale_ref[2 * pair]) * 0.125


def join_pair(wide):
    rows = wide.shape[0] // 2
    second = lax.broadcasted_iota(jnp.int32, (rows, wide.shape[1]), 1) >= HEAD
    return jnp.where(second, wide[rows:], wide[:rows]).astype(BF16)


def inner_kernel(
    scale_ref, shift_ref, ac_ref, b_ref, mid_ref, w_ref, wo_ref, ac_out, mixed_ref, qkv, out
):
    width = ac_ref.shape[1]
    rows = jnp.concatenate([ac_ref[...], b_ref[...]], axis=0)
    for n in range(width // QUAD):
        some = slice(n * QUAD, (n + 1) * QUAD)
        for c in range(3):
            at = c * width + n * QUAD
            part = dot(rows, w_ref[:, at : at + QUAD]).astype(BF16)
            ac_out[c, :, some] = part[:WIN]
            qkv[c, :, some] = part[WIN:]
        for pair in range(n * QUAD // LANES, (n + 1) * QUAD // LANES):
            cols = slice(pair * LANES, (pair + 1) * LANES)
            scores = dot_t(pair_queries(qkv[0, :, cols]), qkv[1, :, cols])
            probs = soft_rows(scores * pair_scale(scale_ref, pair, scores.shape))
            out[:, cols] = join_pair(dot(probs, qkv[2, :, cols]))
    first = lax.broadcasted_iota(jnp.int32, (WIN, QUAD), 0) < shift_ref[0]
    for n in range(width // QUAD):
        some = slice(n * QUAD, (n + 1) * QUAD)
        mid = jnp.where(first, mid_ref[WIN:, some], mid_ref[:WIN, some])
        mixed_ref[:, some] = (mid.astype(F32) + dot(out[...], wo_ref[:, some])).astype(BF16)


def cross_kernel(
    scale_ref, side_ref, shift_ref, near_ref, far_ref, ac_ref, inner_ref, mid_ref, w_ref, wo_ref,
    mixed_ref, keys, values, out,
):
    width = mid_ref.shape[1]
    shift = shift_ref[0]
    first = (lax.broadcasted_iota(jnp.int32, (WIN, width), 0) < shift).astype(jnp.int32)
    halo = jnp.where(first != side_ref[0], near_ref[...], far_ref[...])
    early = lax.broadcasted_iota(jnp.int32, (2 * WIN, WIN), 0) % WIN < shift
    early_key = lax.broadcasted_iota(jnp.int32, (2 * WIN, WIN), 1) < shift
    owned = early.astype(jnp.int32) == early_key.astype(jnp.int32)
    zero = BF16(0)
    for n in range(width // QUAD):
        some = slice(n * QUAD, (n + 1) * QUAD)
        for c, all_rows in enumerate((keys, values)):
            at = (c + 1) * width + n * QUAD
            all_rows[:WIN, some] = ac_ref[c + 1, :, some]
            all_rows[WIN:, some] = dot(halo, w_ref[:, at : at + QUAD]).astype(BF16)
        for pair in range(n * QUAD // LANES, (n + 1) * QUAD // LANES):
            cols = slice(pair * LANES, (pair + 1) * LANES)
            both = dot_t(pair_queries(ac_ref[0, :, cols]), keys[:, cols])
            scores = jnp.where(owned, both[:, :WIN], both[:, WIN:])
            probs = soft_rows(scores * pair_scale(scale_ref, pair, scores.shape))
            wide = jnp.concatenate(
                [jnp.where(owned, probs, zero), jnp.where(owned, zero, probs)], axis=1
            )
            out[:, cols] = join_pair(dot(wide, values[:, cols]))
    upper = lax.broadcasted_iota(jnp.int32, (WIN, QUAD), 0) < shift
    for n in range(width // QUAD):
        some = slice(n * QUAD, (n + 1) * QUAD)
        mid = jnp.where(upper, mid_ref[:WIN, some], mid_ref[WIN:, some])
        mixed = (mid.astype(F32) + dot(out[...], wo_ref[:, some])).astype(BF16)
        inner = inner_ref[:, some]
        mixed_ref[:WIN, some] = jnp.where(upper, mixed, inner)
        mixed_ref[WIN:, some] = jnp.where(upper, inner, mixed)


VMEM = pl.BlockSpec(memory_space=pltpu.VMEM)
SMEM = pl.BlockSpec(memory_space=pltpu.SMEM)
ANY = pl.BlockSpec(memory_space=pl.ANY)
HBM = pl.BlockSpec(memory_space=pltpu.HBM)


def call(kernel, out_shape, in_specs, scratch, mib, flops, moved, name, space=None):
    return pl.pallas_call(
        kernel,
        out_shape=out_shape,
        in_specs=in_specs,
        out_specs=jax.tree.map(lambda _: space or VMEM, out_shape),
        scratch_shapes=scratch,
        compiler_params=pltpu.CompilerParams(vmem_limit_bytes=mib * 2**20),
        cost_estimate=pl.CostEstimate(flops=flops, bytes_accessed=moved, transcendentals=0),
        name=name,
    )


def local(
    grid_features,
    mesh_features,
    sources,
    window_shift,
    w_query,
    w_grid_kv,
    w_enc_out,
    norm_gain,
    w_win_qkv,
    w_win_out,
    head_scale,
):
    grid_rows, width = grid_features.shape
    mesh_rows = mesh_features.shape[0]
    heads = head_scale.shape[0]
    edge_count = sources.shape[1]
    bands = lax.axis_size("band")
    band = lax.axis_index("band")
    side = (band % 2).astype(jnp.int32).reshape(1)
    near = [(i, i ^ 1) for i in range(bands)]
    far = [pair for i in range(1, bands - 1, 2) for pair in ((i, i + 1), (i + 1, i))]
    around = far + [(bands - 1, 0), (0, bands - 1)]
    strip = jax.ShapeDtypeStruct((REACH, width), BF16)
    near_rows, far_rows = call(
        halo_kernel, (strip, strip), [SMEM, HBM],
        [
            pltpu.VMEM((2 * REACH // WIN, WIN, width), BF16),
            pltpu.SemaphoreType.DMA((2 * REACH // WIN,)),
            pltpu.SemaphoreType.DMA((2 * REACH // WIN,)),
        ],
        57, HALO_FLOPS, HALO_BYTES, "halo", HBM,
    )(side, grid_features)
    far_grid = lax.ppermute(far_rows, "band", far)
    near_grid = lax.ppermute(near_rows, "band", near)
    rel = jnp.pad(sources.T - band * grid_rows, ((0, -edge_count % 8), (0, 0)))
    gain = norm_gain.reshape(1, width)

    def arr(*shape, dtype=BF16):
        return jax.ShapeDtypeStruct(shape, dtype)

    full = (mesh_rows, width)
    tile = (WIN, width)
    spread = pltpu.VMEM((heads, mesh_rows, width), BF16)
    total = pltpu.VMEM((heads * RIM, width), F32)
    groups = mesh_rows // RIM
    mid, ac, b, qrim = call(
        functools.partial(interior_kernel, edge_count),
        (arr(*full), arr(*tile), arr(*tile), arr(2, heads * RIM, width)),
        [SMEM, VMEM, HBM, VMEM, HBM, HBM, HBM, VMEM],
        [
            pltpu.VMEM((grid_rows, width), BF16),
            pltpu.VMEM((width, width), BF16),
            pltpu.VMEM((width, 2 * width), BF16),
            pltpu.VMEM((width, width), BF16),
            pltpu.VMEM((mesh_rows, rel.shape[0]), F32),
            spread, spread,
            pltpu.VMEM(full, BF16),
            pltpu.VMEM(full, BF16),
            total,
            pltpu.SMEM((groups,), jnp.int32),
            pltpu.SMEM((groups,), jnp.int32),
            pltpu.SemaphoreType.DMA((5,)),
        ],
        52, 10**10, 3 * 10**7, "interior",
    )(window_shift, rel, grid_features, mesh_features, w_query, w_grid_kv, w_enc_out, gain)

    mid, ac, b = call(
        functools.partial(rim_kernel, edge_count),
        (arr(*full), arr(*tile), arr(*tile)),
        [SMEM, SMEM, VMEM, ANY, ANY, HBM, ANY, VMEM, HBM, HBM] + [VMEM] * 4,
        [
            pltpu.VMEM((2, grid_rows + REACH, width), BF16),
            pltpu.VMEM((2, heads * RIM, width), BF16),
            pltpu.VMEM((width, width), BF16),
            pltpu.VMEM((width, width), BF16),
            pltpu.VMEM((heads, 2 * RIM, width), BF16),
            pltpu.VMEM((2 * RIM, width), BF16),
            total,
            pltpu.SemaphoreType.DMA((7,)),
        ],
        50, 10**9, 10**7, "rims",
    )(
        side, window_shift, rel, near_grid, far_grid, grid_features, qrim, mesh_features,
        w_grid_kv, w_enc_out, gain, mid, ac, b,
    )

    far_norm = lax.ppermute(ac, "band", around)
    near_norm = lax.ppermute(ac, "band", near)

    qkv_ac, inner = call(
        inner_kernel,
        (arr(3, *tile), arr(*tile)),
        [SMEM, SMEM] + [VMEM] * 5,
        [pltpu.VMEM((3, *tile), BF16), pltpu.VMEM(tile, BF16)],
        16, 2 * 10**9, 10**7, "inner",
    )(head_scale, window_shift, ac, b, mid, w_win_qkv, w_win_out)

    return call(
        cross_kernel,
        arr(*full),
        [SMEM] * 3 + [VMEM] * 7,
        [
            pltpu.VMEM((2 * WIN, width), BF16),
            pltpu.VMEM((2 * WIN, width), BF16),
            pltpu.VMEM(tile, BF16),
        ],
        16, 2 * 10**9, 10**7, "cross",
    )(
        head_scale, side, window_shift, near_norm, far_norm, qkv_ac, inner, mid,
        w_win_qkv, w_win_out,
    )


def solution(mesh):
    placed = (P("band", None),) * 3 + (P(),) * 8
    return jax.shard_map(
        local, mesh=mesh, in_specs=placed, out_specs=P("band", None), check_vma=False
    )
```

```python
import functools

import jax
import jax.numpy as jnp
from jax import lax
from jax.experimental import pallas as pl
from jax.experimental.pallas import tpu as pltpu
from jax.sharding import PartitionSpec as P

WIN = 128
REACH = 384
RIM = 16
HEAD = 64
QUAD = 256
LANES = 128
NEG = -1e30
HALO_FLOPS = 10**10
HALO_BYTES = 3 * 10**7

BF16 = jnp.bfloat16
F32 = jnp.float32


def dot(a, b):
    return jnp.dot(a, b, preferred_element_type=F32)


def dot_t(a, b):
    return lax.dot_general(a, b, (((1,), (1,)), ((), ())), preferred_element_type=F32)


def layer_norm(mid, gain):
    wide = mid.astype(F32)
    center = jnp.mean(wide, axis=-1, keepdims=True)
    spread = jnp.mean((wide - center) ** 2, axis=-1, keepdims=True)
    return ((wide - center) / jnp.sqrt(spread + 1e-05) * gain).astype(BF16)


def count_edges(rel, start, cols):
    nodes, edge_count = rel.shape
    row = (lax.broadcasted_iota(jnp.int32, (nodes, cols), 1) + start).astype(F32)
    total = jnp.zeros((nodes, cols), F32)
    for e in range(edge_count):
        total += (rel[:, e : e + 1] == row).astype(F32)
    return total


def by_node(values):
    return values.reshape(values.shape[0] // RIM, RIM, values.shape[1])


def masked_scores(queries, rows, count):
    return by_node(dot_t(queries, rows)) + jnp.where(count > 0, 0.0, NEG)[None]


def row_weights(queries, rows, count):
    scores = masked_scores(queries, rows, count)
    top = jnp.max(scores, axis=-1, keepdims=True)
    grown = jnp.exp(scores - top) * count[None]
    weights = grown / jnp.sum(grown, axis=-1, keepdims=True)
    return weights.reshape(queries.shape[0], rows.shape[0]).astype(BF16)


def attend_all(queries, rel, rows_ref, total_ref):
    blocks = rows_ref.shape[0] // WIN
    heads = queries.shape[0] // RIM

    def block(i):
        at = pl.multiple_of(i * WIN, WIN)
        rows = rows_ref[pl.ds(at, WIN), :]
        count = count_edges(rel, at, WIN)
        return rows, count, masked_scores(queries, rows, count)

    def find(i, carry):
        top, size = carry
        _, count, scores = block(i)
        new = jnp.maximum(top, jnp.max(scores, axis=-1, keepdims=True))
        part = jnp.sum(jnp.exp(scores - new) * count[None], axis=-1, keepdims=True)
        return new, size * jnp.exp(top - new) + part

    start = (jnp.full((heads, RIM, 1), NEG, F32), jnp.zeros((heads, RIM, 1), F32))
    top, size = lax.fori_loop(0, blocks, find, start)
    total_ref[...] = jnp.zeros(total_ref.shape, F32)

    def add(i, carry):
        rows, count, scores = block(i)
        weights = jnp.exp(scores - top) * count[None] / size
        total_ref[...] += dot(weights.reshape(heads * RIM, WIN).astype(BF16), rows)
        return carry

    lax.fori_loop(0, blocks, add, 0)
    return total_ref[...].astype(BF16)


def project_heads(pool, w_ref, out_ref, quad):
    per, rows, width = pool.shape
    cols = pl.ds(pl.multiple_of(quad * QUAD, QUAD), QUAD)
    wide = dot(pool.reshape(per * rows, width), w_ref[:, cols])
    head = lax.broadcasted_iota(jnp.int32, (rows, QUAD), 1) // HEAD
    total = wide[:rows]
    for j in range(1, per):
        total = jnp.where(head == j, wide[j * rows : (j + 1) * rows], total)
    out_ref[:, cols] = total.astype(BF16)


def halo_kernel(side_ref, x_hbm, near_hbm, far_hbm, held, in_sems, out_sems):
    rows = near_hbm.shape[0]
    tail = x_hbm.shape[0] - rows
    near_at = jnp.where(side_ref[0] == 0, tail, 0)
    fetches, sends = [], []
    for i, (at, target) in enumerate(((tail - near_at, far_hbm), (near_at, near_hbm))):
        for k in range(rows // WIN):
            n = i * (rows // WIN) + k
            place = pl.ds(pl.multiple_of(at + k * WIN, WIN), WIN)
            target_rows = target.at[pl.ds(k * WIN, WIN)]
            fetches.append(pltpu.make_async_copy(x_hbm.at[place], held.at[n], in_sems.at[n]))
            sends.append(pltpu.make_async_copy(held.at[n], target_rows, out_sems.at[n]))
    for fetch in fetches:
        fetch.start()
    for fetch, send in zip(fetches, sends):
        fetch.wait()
        send.start()
    for send in sends:
        send.wait()


def interior_kernel(
    edge_count, shift_ref, edge_ref, x_hbm, mesh_ref, wq_hbm, wkv_hbm, we_hbm, gain_ref,
    mid_ref, ac_ref, b_ref, qrim_ref,
    x_ref, wq_ref, wkv_ref, we_ref,
    rel_ref, pool, pooled, qs, gathered, total_ref, begin_ref, fits_ref, sems,
):
    width = mesh_ref.shape[1]
    key_cols, value_cols = pl.ds(0, width), pl.ds(width, width)
    copies = [
        pltpu.make_async_copy(source, target, sems.at[i])
        for i, (source, target) in enumerate(
            (
                (wq_hbm, wq_ref),
                (wkv_hbm.at[:, key_cols], wkv_ref.at[:, key_cols]),
                (x_hbm, x_ref),
                (wkv_hbm.at[:, value_cols], wkv_ref.at[:, value_cols]),
                (we_hbm, we_ref),
            )
        )
    ]
    for copy in copies:
        copy.start()
    heads, mesh_rows, width = pool.shape
    grid_rows = x_ref.shape[0]
    quads = width // QUAD
    groups = mesh_rows // RIM
    rel_ref[...] = edge_ref[...].astype(F32).T
    for group in range(1, groups - 1):
        rel = rel_ref[group * RIM : (group + 1) * RIM, :edge_count]
        low = jnp.min(rel).astype(jnp.int32)
        high = jnp.max(rel).astype(jnp.int32)
        begin = jnp.clip(low // 16 * 16, 0, grid_rows - QUAD)
        begin_ref[group] = begin
        fits_ref[group] = (high - begin < QUAD).astype(jnp.int32)
    copies[0].wait()
    for n in range(quads):
        cols = slice(n * QUAD, (n + 1) * QUAD)
        qs[:, cols] = dot(mesh_ref[...], wq_ref[:, cols]).astype(BF16) * BF16(0.125)

    def key_step(t, carry):
        cols = pl.ds(pl.multiple_of(t * QUAD, QUAD), QUAD)
        queries = qs[:, cols]
        head = lax.broadcasted_iota(jnp.int32, queries.shape, 1) // HEAD
        own = jnp.concatenate([jnp.where(head == j, queries, BF16(0)) for j in range(4)], axis=0)
        for n in range(quads):
            some = slice(n * QUAD, (n + 1) * QUAD)
            part = dot_t(own, wkv_ref[some, cols]).astype(BF16)
            pool[pl.ds(t * 4, 4), :, some] = part.reshape(4, mesh_rows, QUAD)
        return carry

    copies[1].wait()
    lax.fori_loop(0, quads, key_step, 0, unroll=4)
    copies[2].wait()
    for side, group in enumerate((0, groups - 1)):
        rows = slice(group * RIM, (group + 1) * RIM)
        qrim_ref[side] = pool[:, rows, :].reshape(heads * RIM, width)
        pooled[:, rows, :] = jnp.zeros((heads, RIM, width), BF16)

    def rows_of(group):
        return pl.ds(pl.multiple_of(group * RIM, RIM), RIM)

    def queries_of(group):
        return pool[:, rows_of(group), :].reshape(heads * RIM, width)

    def put(group, part):
        pooled[:, rows_of(group), :] = part.reshape(heads, RIM, width)

    def group_step(i, carry):
        for k in range(2):
            group = 1 + 2 * i + k
            begin = pl.multiple_of(begin_ref[group], 16)
            rows = x_ref[pl.ds(begin, QUAD), :]
            count = count_edges(rel_ref[rows_of(group), :edge_count], begin, QUAD)
            weights = row_weights(queries_of(group), rows, count)
            put(group, dot(weights, rows).astype(BF16))
        return carry

    lax.fori_loop(0, (groups - 2) // 2, group_step, 0, unroll=7)

    def check_step(group, carry):
        @pl.when(fits_ref[group] == 0)
        def _():
            rel = rel_ref[rows_of(group), :edge_count]
            put(group, attend_all(queries_of(group), rel, x_ref, total_ref))

        return carry

    lax.fori_loop(1, groups - 1, check_step, 0)

    def value_step(t, carry):
        project_heads(pooled[pl.ds(t * 4, 4)], wkv_ref.at[:, width:], gathered, t)
        return carry

    copies[3].wait()
    lax.fori_loop(0, quads, value_step, 0, unroll=4)
    copies[4].wait()
    for n in range(quads):
        cols = slice(n * QUAD, (n + 1) * QUAD)
        total = mesh_ref[:, cols].astype(F32) + dot(gathered[...], we_ref[:, cols])
        mid_ref[:, cols] = total.astype(BF16)
    norm = layer_norm(mid_ref[...], gain_ref[...])
    first = lax.broadcasted_iota(jnp.int32, (WIN, width), 0) < shift_ref[0]
    ac_ref[...] = jnp.where(first, norm[:WIN], norm[WIN:])
    b_ref[...] = jnp.where(first, norm[WIN:], norm[:WIN])


def rim_kernel(
    edge_count, side_ref, shift_ref, edge_ref, near_hbm, far_hbm, x_hbm, qrim_hbm, mesh_ref, wkv_hbm, we_hbm,
    gain_ref, mid_in, ac_in, b_in,
    mid_ref, ac_ref, b_ref,
    held, qrim_ref, wv_ref, we_ref, pool, gathered, total_ref, sems,
):
    mesh_rows, width = mid_ref.shape
    get_wv = pltpu.make_async_copy(wkv_hbm.at[:, pl.ds(width, width)], wv_ref, sems.at[5])
    get_we = pltpu.make_async_copy(we_hbm, we_ref, sems.at[6])
    grid_rows = x_hbm.shape[0]
    heads = pool.shape[0]
    quads = width // QUAD
    wide = REACH + WIN
    tail = grid_rows - WIN
    held_low, held_high = held.at[0], held.at[1]
    side = side_ref[0]
    copies = [
        pltpu.make_async_copy(qrim_hbm, qrim_ref, sems.at[0]),
        pltpu.make_async_copy(
            x_hbm.at[pl.ds(0, WIN)], held_low.at[pl.ds(REACH, WIN)], sems.at[1]
        ),
        pltpu.make_async_copy(
            x_hbm.at[pl.ds(tail, WIN)], held_high.at[pl.ds(tail, WIN)], sems.at[2]
        ),
    ]
    for i, (end, source) in enumerate(((side, far_hbm), (1 - side, near_hbm))):
        rows = pl.ds(pl.multiple_of(end * grid_rows, WIN), REACH)
        copies.append(pltpu.make_async_copy(source, held.at[end, rows], sems.at[3 + i]))
    for copy in copies:
        copy.start()
    get_wv.start()
    get_we.start()
    rel = edge_ref[...].astype(F32).T
    rel_low = rel[:RIM, :edge_count] + float(REACH)
    rel_high = rel[mesh_rows - RIM :, :edge_count]
    count_low = count_edges(rel_low, 0, wide)
    count_high = count_edges(rel_high, tail, wide)
    fits = jnp.max(rel_low) < wide
    fits_high = jnp.min(rel_high) >= tail
    for copy in copies:
        copy.wait()

    def put(side, part):
        pool[:, side * RIM : (side + 1) * RIM, :] = part.reshape(heads, RIM, width)

    weights_low = row_weights(qrim_ref[0], held_low[:wide], count_low)
    weights_high = row_weights(qrim_ref[1], held_high[tail:], count_high)
    put(0, dot(weights_low, held_low[:wide]).astype(BF16))
    put(1, dot(weights_high, held_high[tail:]).astype(BF16))

    @pl.when(jnp.logical_not(jnp.logical_and(fits, fits_high)))
    def _():
        whole_low = pltpu.make_async_copy(x_hbm, held_low.at[pl.ds(REACH, grid_rows)], sems.at[0])
        whole_high = pltpu.make_async_copy(x_hbm, held_high.at[pl.ds(0, grid_rows)], sems.at[1])
        whole_low.start()
        whole_high.start()
        whole_low.wait()
        whole_high.wait()
        put(0, attend_all(qrim_ref[0], rel_low, held_low, total_ref))
        put(1, attend_all(qrim_ref[1], rel_high, held_high, total_ref))

    get_wv.wait()
    for t in range(quads):
        project_heads(pool[t * 4 : (t + 1) * 4], wv_ref, gathered, t)
    get_we.wait()
    edge_mesh = jnp.concatenate([mesh_ref[:RIM], mesh_ref[mesh_rows - RIM :]], axis=0)
    rim_mid = (edge_mesh.astype(F32) + dot(gathered[...], we_ref[...])).astype(BF16)
    rim_norm = layer_norm(rim_mid, gain_ref[...])
    inside = slice(RIM, mesh_rows - RIM)
    mid_ref[inside] = mid_in[inside]
    inside = slice(RIM, WIN - RIM)
    ac_ref[inside] = ac_in[inside]
    b_ref[inside] = b_in[inside]
    row = lax.broadcasted_iota(jnp.int32, (RIM, width), 0)
    for side in range(2):
        part = slice(side * RIM, (side + 1) * RIM)
        at = slice(side * (mesh_rows - RIM), side * (mesh_rows - RIM) + RIM)
        mid_ref[at] = rim_mid[part]
        at = slice(side * (WIN - RIM), side * (WIN - RIM) + RIM)
        crosses = (row + at.start < shift_ref[0]).astype(jnp.int32) != side
        ac_ref[at] = jnp.where(crosses, rim_norm[part], ac_in[at])
        b_ref[at] = jnp.where(crosses, b_in[at], rim_norm[part])


def soft_rows(scores):
    top = jnp.max(scores, axis=-1, keepdims=True)
    grown = jnp.exp(scores - top)
    return (grown / jnp.sum(grown, axis=-1, keepdims=True)).astype(BF16)


def pair_queries(queries):
    second = lax.broadcasted_iota(jnp.int32, queries.shape, 1) >= HEAD
    zero = BF16(0)
    return jnp.concatenate(
        [jnp.where(second, zero, queries), jnp.where(second, queries, zero)], axis=0
    )


def pair_scale(scale_ref, pair, shape):
    upper = lax.broadcasted_iota(jnp.int32, shape, 0) >= shape[0] // 2
    return jnp.where(upper, scale_ref[2 * pair + 1], scale_ref[2 * pair]) * 0.125


def join_pair(wide):
    rows = wide.shape[0] // 2
    second = lax.broadcasted_iota(jnp.int32, (rows, wide.shape[1]), 1) >= HEAD
    return jnp.where(second, wide[rows:], wide[:rows]).astype(BF16)


def inner_kernel(
    scale_ref, shift_ref, ac_ref, b_ref, mid_ref, w_ref, wo_ref, ac_out, mixed_ref, qkv, out
):
    width = ac_ref.shape[1]
    rows = jnp.concatenate([ac_ref[...], b_ref[...]], axis=0)
    for n in range(width // QUAD):
        some = slice(n * QUAD, (n + 1) * QUAD)
        for c in range(3):
            at = c * width + n * QUAD
            part = dot(rows, w_ref[:, at : at + QUAD]).astype(BF16)
            ac_out[c, :, some] = part[:WIN]
            qkv[c, :, some] = part[WIN:]
        for pair in range(n * QUAD // LANES, (n + 1) * QUAD // LANES):
            cols = slice(pair * LANES, (pair + 1) * LANES)
            scores = dot_t(pair_queries(qkv[0, :, cols]), qkv[1, :, cols])
            probs = soft_rows(scores * pair_scale(scale_ref, pair, scores.shape))
            out[:, cols] = join_pair(dot(probs, qkv[2, :, cols]))
    first = lax.broadcasted_iota(jnp.int32, (WIN, QUAD), 0) < shift_ref[0]
    for n in range(width // QUAD):
        some = slice(n * QUAD, (n + 1) * QUAD)
        mid = jnp.where(first, mid_ref[WIN:, some], mid_ref[:WIN, some])
        mixed_ref[:, some] = (mid.astype(F32) + dot(out[...], wo_ref[:, some])).astype(BF16)


def cross_kernel(
    scale_ref, side_ref, shift_ref, near_ref, far_ref, ac_ref, inner_ref, mid_ref, w_ref, wo_ref,
    mixed_ref, keys, values, out,
):
    width = mid_ref.shape[1]
    shift = shift_ref[0]
    first = (lax.broadcasted_iota(jnp.int32, (WIN, width), 0) < shift).astype(jnp.int32)
    halo = jnp.where(first != side_ref[0], near_ref[...], far_ref[...])
    early = lax.broadcasted_iota(jnp.int32, (2 * WIN, WIN), 0) % WIN < shift
    early_key = lax.broadcasted_iota(jnp.int32, (2 * WIN, WIN), 1) < shift
    owned = early.astype(jnp.int32) == early_key.astype(jnp.int32)
    zero = BF16(0)
    for n in range(width // QUAD):
        some = slice(n * QUAD, (n + 1) * QUAD)
        for c, all_rows in enumerate((keys, values)):
            at = (c + 1) * width + n * QUAD
            all_rows[:WIN, some] = ac_ref[c + 1, :, some]
            all_rows[WIN:, some] = dot(halo, w_ref[:, at : at + QUAD]).astype(BF16)
    for n in range(width // QUAD):
        for pair in range(n * QUAD // LANES, (n + 1) * QUAD // LANES):
            cols = slice(pair * LANES, (pair + 1) * LANES)
            both = dot_t(pair_queries(ac_ref[0, :, cols]), keys[:, cols])
            scores = jnp.where(owned, both[:, :WIN], both[:, WIN:])
            probs = soft_rows(scores * pair_scale(scale_ref, pair, scores.shape))
            wide = jnp.concatenate(
                [jnp.where(owned, probs, zero), jnp.where(owned, zero, probs)], axis=1
            )
            out[:, cols] = join_pair(dot(wide, values[:, cols]))
    upper = lax.broadcasted_iota(jnp.int32, (WIN, QUAD), 0) < shift
    for n in range(width // QUAD):
        some = slice(n * QUAD, (n + 1) * QUAD)
        mid = jnp.where(upper, mid_ref[:WIN, some], mid_ref[WIN:, some])
        mixed = (mid.astype(F32) + dot(out[...], wo_ref[:, some])).astype(BF16)
        inner = inner_ref[:, some]
        mixed_ref[:WIN, some] = jnp.where(upper, mixed, inner)
        mixed_ref[WIN:, some] = jnp.where(upper, inner, mixed)


VMEM = pl.BlockSpec(memory_space=pltpu.VMEM)
SMEM = pl.BlockSpec(memory_space=pltpu.SMEM)
ANY = pl.BlockSpec(memory_space=pl.ANY)
HBM = pl.BlockSpec(memory_space=pltpu.HBM)


def call(kernel, out_shape, in_specs, scratch, mib, flops, moved, name, space=None):
    return pl.pallas_call(
        kernel,
        out_shape=out_shape,
        in_specs=in_specs,
        out_specs=jax.tree.map(lambda _: space or VMEM, out_shape),
        scratch_shapes=scratch,
        compiler_params=pltpu.CompilerParams(vmem_limit_bytes=mib * 2**20),
        cost_estimate=pl.CostEstimate(flops=flops, bytes_accessed=moved, transcendentals=0),
        name=name,
    )


def local(
    grid_features,
    mesh_features,
    sources,
    window_shift,
    w_query,
    w_grid_kv,
    w_enc_out,
    norm_gain,
    w_win_qkv,
    w_win_out,
    head_scale,
):
    grid_rows, width = grid_features.shape
    mesh_rows = mesh_features.shape[0]
    heads = head_scale.shape[0]
    edge_count = sources.shape[1]
    bands = lax.axis_size("band")
    band = lax.axis_index("band")
    side = (band % 2).astype(jnp.int32).reshape(1)
    near = [(i, i ^ 1) for i in range(bands)]
    far = [pair for i in range(1, bands - 1, 2) for pair in ((i, i + 1), (i + 1, i))]
    around = far + [(bands - 1, 0), (0, bands - 1)]
    strip = jax.ShapeDtypeStruct((REACH, width), BF16)
    near_rows, far_rows = call(
        halo_kernel, (strip, strip), [SMEM, HBM],
        [
            pltpu.VMEM((2 * REACH // WIN, WIN, width), BF16),
            pltpu.SemaphoreType.DMA((2 * REACH // WIN,)),
            pltpu.SemaphoreType.DMA((2 * REACH // WIN,)),
        ],
        57, HALO_FLOPS, HALO_BYTES, "halo", HBM,
    )(side, grid_features)
    far_grid = lax.ppermute(far_rows, "band", far)
    near_grid = lax.ppermute(near_rows, "band", near)
    rel = jnp.pad(sources.T - band * grid_rows, ((0, -edge_count % 8), (0, 0)))
    gain = norm_gain.reshape(1, width)

    def arr(*shape, dtype=BF16):
        return jax.ShapeDtypeStruct(shape, dtype)

    full = (mesh_rows, width)
    tile = (WIN, width)
    spread = pltpu.VMEM((heads, mesh_rows, width), BF16)
    total = pltpu.VMEM((heads * RIM, width), F32)
    groups = mesh_rows // RIM
    mid, ac, b, qrim = call(
        functools.partial(interior_kernel, edge_count),
        (arr(*full), arr(*tile), arr(*tile), arr(2, heads * RIM, width)),
        [SMEM, VMEM, HBM, VMEM, HBM, HBM, HBM, VMEM],
        [
            pltpu.VMEM((grid_rows, width), BF16),
            pltpu.VMEM((width, width), BF16),
            pltpu.VMEM((width, 2 * width), BF16),
            pltpu.VMEM((width, width), BF16),
            pltpu.VMEM((mesh_rows, rel.shape[0]), F32),
            spread, spread,
            pltpu.VMEM(full, BF16),
            pltpu.VMEM(full, BF16),
            total,
            pltpu.SMEM((groups,), jnp.int32),
            pltpu.SMEM((groups,), jnp.int32),
            pltpu.SemaphoreType.DMA((5,)),
        ],
        52, 10**10, 3 * 10**7, "interior",
    )(window_shift, rel, grid_features, mesh_features, w_query, w_grid_kv, w_enc_out, gain)

    mid, ac, b = call(
        functools.partial(rim_kernel, edge_count),
        (arr(*full), arr(*tile), arr(*tile)),
        [SMEM, SMEM, VMEM, ANY, ANY, HBM, ANY, VMEM, HBM, HBM] + [VMEM] * 4,
        [
            pltpu.VMEM((2, grid_rows + REACH, width), BF16),
            pltpu.VMEM((2, heads * RIM, width), BF16),
            pltpu.VMEM((width, width), BF16),
            pltpu.VMEM((width, width), BF16),
            pltpu.VMEM((heads, 2 * RIM, width), BF16),
            pltpu.VMEM((2 * RIM, width), BF16),
            total,
            pltpu.SemaphoreType.DMA((7,)),
        ],
        50, 10**9, 10**7, "rims",
    )(
        side, window_shift, rel, near_grid, far_grid, grid_features, qrim, mesh_features,
        w_grid_kv, w_enc_out, gain, mid, ac, b,
    )

    far_norm = lax.ppermute(ac, "band", around)
    near_norm = lax.ppermute(ac, "band", near)

    qkv_ac, inner = call(
        inner_kernel,
        (arr(3, *tile), arr(*tile)),
        [SMEM, SMEM] + [VMEM] * 5,
        [pltpu.VMEM((3, *tile), BF16), pltpu.VMEM(tile, BF16)],
        16, 2 * 10**9, 10**7, "inner",
    )(head_scale, window_shift, ac, b, mid, w_win_qkv, w_win_out)

    return call(
        cross_kernel,
        arr(*full),
        [SMEM] * 3 + [VMEM] * 7,
        [
            pltpu.VMEM((2 * WIN, width), BF16),
            pltpu.VMEM((2 * WIN, width), BF16),
            pltpu.VMEM(tile, BF16),
        ],
        16, 2 * 10**9, 10**7, "cross",
    )(
        head_scale, side, window_shift, near_norm, far_norm, qkv_ac, inner, mid,
        w_win_qkv, w_win_out,
    )


def solution(mesh):
    placed = (P("band", None),) * 3 + (P(),) * 8
    return jax.shard_map(
        local, mesh=mesh, in_specs=placed, out_specs=P("band", None), check_vma=False
    )
```
